128 devices in a mesh: grp: 2 (over x_hi), seq: 16 (over x_lo, y, core), dp: 4 (over z).
Axes of the slice: x: 4 (x_hi: 2, x_lo: 2; x = x_hi * 2 + x_lo), y: 4, z: 4, core: 2. Of those that a mesh axis runs over, the one named last changes fastest.
Arguments:
- text_states: bfloat16 [4, 256, 4096], P('dp', 'grp'), may hold values from -6 to 6
- text_lengths: int32 [4], P('dp'), may hold values from 32 to 256, as said below
- norm_gain: float32 [4096], replicated, may hold values from 0.1 to 1.9
- final_gain: float32 [4096], replicated, may hold values from 0.1 to 1.9
- wi_gate: bfloat16 [4096, 10240], P(None, 'seq'), may hold values from -0.09375 to 0.09375
- wi_up: bfloat16 [4096, 10240], P(None, 'seq'), may hold values from -0.09375 to 0.09375
- wo_weight: bfloat16 [10240, 4096], P('seq'), may hold values from -0.0625 to 0.0625
- text_proj: bfloat16 [4096, 6144], P(None, 'seq'), may hold values from -0.09375 to 0.09375
- image_qkv: bfloat16 [4, 4096, 6144], P('dp', ('grp', 'seq')), may hold values from -56 to 56
- image_cot: bfloat16 [4, 4096, 2048], P('dp', ('grp', 'seq')), may hold values from -96 to 96
- text_cot: bfloat16 [4, 256, 2048], P('dp', 'grp', 'seq'), may hold values from -96 to 96
Outputs:
- image_grads: bfloat16 [4, 4096, 6144], P('dp', 'grp', 'seq')
- proj_grad: float32 [4096, 6144], P(('grp', 'dp'), 'seq')
The draws below stay inside these ranges and needn't reach their ends.
Inputs may be any that keep to these rules, and one draw needn't show every extreme that they name: `text_lengths`: one sample has all 256 text tokens and one has 32.
All inputs are finite; a program needn't handle non-finite values.
Results may differ from the reference program's by a relative error of at most 0.023.
Values may be sent and summed in bfloat16 or wider, within the bound.
No kernel may reach another device: no remote copies, remote signals or barrier semaphores. Data moves between devices by JAX's collectives and lax.ppermute only.
A program may use at most 192 MiB of HBM per device.

```python
import jax
import jax.numpy as jnp
from jax import lax

T5_WIDTH = 4096
ENC_HIDDEN = 10240
ATTN_HEADS = 32
HEAD_DIM = 64
TEXT_LEN = 256
IMAGE_LEN = 4096
SAMPLES = 4


def draw_text_lengths(key, part):
    key = jax.random.fold_in(key, 5)
    first_key, second_key = jax.random.split(key)
    drawn = jax.random.randint(first_key, (SAMPLES,), TEXT_LEN // 8, TEXT_LEN + 1, dtype=jnp.int32)
    order = jax.random.permutation(second_key, SAMPLES)
    return drawn.at[order[0]].set(TEXT_LEN).at[order[1]].set(TEXT_LEN // 8)


def draw_image_qkv(key, part):
    key = jax.random.fold_in(key, 11)
    shape = (SAMPLES, IMAGE_LEN, ATTN_HEADS, 3, HEAD_DIM)
    base = jnp.clip(jax.random.normal(key, shape, jnp.float32), -4.0, 4.0)
    return base.reshape(SAMPLES, IMAGE_LEN, ATTN_HEADS * 3 * HEAD_DIM).astype(jnp.bfloat16)


def block_levels(stream_key, extent, pieces, low, high):
    gain = 1.0
    for dim, parts in pieces:
        steps = jax.random.uniform(jax.random.fold_in(jax.random.fold_in(stream_key, 6), dim), (parts,), jnp.float32, low / len(pieces), high / len(pieces))
        gain = gain * jnp.repeat(jnp.exp(steps), extent[dim] // parts).reshape((-1,) + (1,) * (len(extent) - 1 - dim))
    return gain


def bell_draw(key, shape, width, bound, shards=(), kind=jnp.bfloat16):
    values = width * jax.random.normal(key, shape, jnp.float32)
    if shards:
        values = values * block_levels(key, shape, shards, -0.22, 0.18)
    return jnp.clip(values, -bound, bound).astype(kind)


def setup_inputs(seed: int = 0) -> dict:
    streams_of = jax.random.split(jax.random.key(seed), 12)
    return {
        "text_states": bell_draw(streams_of[0], (SAMPLES, TEXT_LEN, T5_WIDTH), 1.0, 6.0, ((0, 4), (1, 2))),
        "text_lengths": draw_text_lengths(jax.random.fold_in(streams_of[11], 71), 0),
        "norm_gain": jnp.clip(1.0 + 0.18 * jax.random.normal(streams_of[2], (T5_WIDTH,), jnp.float32), 0.1, 1.9),
        "final_gain": jnp.clip(1.0 + 0.18 * jax.random.normal(streams_of[3], (T5_WIDTH,), jnp.float32), 0.1, 1.9),
        "wi_gate": bell_draw(streams_of[4], (T5_WIDTH, ENC_HIDDEN), T5_WIDTH ** -0.5, 0.09375, ((1, 16),)),
        "wi_up": bell_draw(streams_of[5], (T5_WIDTH, ENC_HIDDEN), T5_WIDTH ** -0.5, 0.09375, ((1, 16),)),
        "wo_weight": bell_draw(streams_of[6], (ENC_HIDDEN, T5_WIDTH), ENC_HIDDEN ** -0.5, 0.0625, ((0, 16),)),
        "text_proj": bell_draw(streams_of[7], (T5_WIDTH, ATTN_HEADS * 3 * HEAD_DIM), T5_WIDTH ** -0.5, 0.09375, ((1, 16),)),
        "image_qkv": draw_image_qkv(jax.random.fold_in(streams_of[11], 71), 0),
        "image_cot": bell_draw(streams_of[9], (SAMPLES, IMAGE_LEN, ATTN_HEADS * HEAD_DIM), 16.0, 96.0, ((0, 4), (1, 32))),
        "text_cot": bell_draw(streams_of[10], (SAMPLES, TEXT_LEN, ATTN_HEADS * HEAD_DIM), 16.0, 96.0, ((0, 4), (1, 2), (2, 16))),
    }


def rms_norm(values_in, norm_scale):
    mean_sq = lax.optimization_barrier(jnp.mean(values_in * values_in, axis=-1, keepdims=True))
    return values_in * lax.rsqrt(mean_sq + 1e-06) * norm_scale

def head_grads(query, key_in, value_in, cot, key_valid):
    scale = HEAD_DIM ** (-0.5)
    scores = jnp.dot(query, key_in.T, preferred_element_type=jnp.float32) * scale
    scores = jnp.where(key_valid[None, :], scores, jnp.float32(-1e+30))
    top = lax.optimization_barrier(jnp.max(scores, axis=-1, keepdims=True))
    expo = jnp.exp(scores - top)
    probs = expo / lax.optimization_barrier(jnp.sum(expo, axis=-1, keepdims=True))
    probs_low = probs.astype(jnp.bfloat16)
    attn = jnp.dot(probs_low, value_in, preferred_element_type=jnp.float32)
    delta = lax.optimization_barrier(jnp.sum(cot.astype(jnp.float32) * attn, axis=-1, keepdims=True))
    dprobs = jnp.dot(cot, value_in.T, preferred_element_type=jnp.float32)
    dscores = (probs * (dprobs - delta) * scale).astype(jnp.bfloat16)
    grad_v = jnp.dot(probs_low.T, cot, preferred_element_type=jnp.float32)
    grad_k = jnp.dot(dscores.T, query, preferred_element_type=jnp.float32)
    grad_q = jnp.dot(dscores, key_in, preferred_element_type=jnp.float32)
    return jnp.stack([grad_q, grad_k, grad_v], axis=1).astype(jnp.bfloat16)

def reference(text_states, text_lengths, norm_gain, final_gain, wi_gate, wi_up, wo_weight, text_proj, image_qkv, image_cot, text_cot):
    key_count = TEXT_LEN + IMAGE_LEN
    position = jnp.arange(key_count, dtype=jnp.int32)
    image_list = []
    proj_grad = jnp.zeros((T5_WIDTH, ATTN_HEADS * 3 * HEAD_DIM), jnp.float32)
    for sample in range(SAMPLES):
        states = text_states[sample]
        normed = rms_norm(states.astype(jnp.float32), norm_gain).astype(jnp.bfloat16)
        gate_act = jnp.dot(normed, wi_gate, preferred_element_type=jnp.float32)
        up_act = jnp.dot(normed, wi_up, preferred_element_type=jnp.float32)
        hidden = (jax.nn.gelu(gate_act, approximate=True) * up_act).astype(jnp.bfloat16)
        encoded = states.astype(jnp.float32) + jnp.dot(hidden, wo_weight, preferred_element_type=jnp.float32)
        text_final = rms_norm(encoded, final_gain).astype(jnp.bfloat16)
        text_qkv = jnp.dot(text_final, text_proj, preferred_element_type=jnp.float32).astype(jnp.bfloat16)
        joint = jnp.concatenate([text_qkv, image_qkv[sample]], axis=0).reshape(key_count, ATTN_HEADS, 3, HEAD_DIM)
        joint_cot = jnp.concatenate([text_cot[sample], image_cot[sample]], axis=0).reshape(key_count, ATTN_HEADS, HEAD_DIM)
        key_valid = (position >= TEXT_LEN) | (position < text_lengths[sample])
        per_head = jnp.moveaxis(joint, 1, 0)
        cot_heads = jnp.moveaxis(joint_cot, 1, 0)

        def one_head(pair):
            head_qkv, head_cot = pair
            return head_grads(head_qkv[:, 0], head_qkv[:, 1], head_qkv[:, 2], head_cot, key_valid)
        grads = lax.map(one_head, (per_head, cot_heads))
        joint_grads = jnp.moveaxis(grads, 0, 1).reshape(key_count, ATTN_HEADS * 3 * HEAD_DIM)
        image_list.append(joint_grads[TEXT_LEN:])
        proj_grad = proj_grad + lax.dot_general(text_final, joint_grads[:TEXT_LEN], (((0,), (0,)), ((), ())), preferred_element_type=jnp.float32)
    return (jnp.stack(image_list, axis=0), proj_grad)
```

```python
import functools

import jax
import jax.numpy as jnp
from jax import lax
from jax.experimental import pallas as pl
from jax.experimental.pallas import tpu as pltpu
from jax.sharding import PartitionSpec as P

f32, bf16 = jnp.float32, jnp.bfloat16
HD = 64
QB = 256
LOG2E_SCALED = 1.4426950408889634 / 8.0
VMEM_LIMIT = 50 << 20


def dot(a, b, ca, cb):
    return lax.dot_general(a, b, (((ca,), (cb,)), ((), ())), preferred_element_type=f32)


def fold8(x, op):
    return op(x.reshape(x.shape[0] // 8, 8, x.shape[1]), axis=0)


def params(limit=VMEM_LIMIT):
    return pltpu.CompilerParams(vmem_limit_bytes=limit)


def cost(flops, nbytes, trans=0):
    return pl.CostEstimate(flops=int(flops), bytes_accessed=int(nbytes), transcendentals=int(trans))


def full_spec(shape):
    return pl.BlockSpec(shape, lambda i, *_: (0,) * len(shape))


def halves(blk):
    lane = lax.broadcasted_iota(jnp.int32, blk.shape, 1)
    zero = jnp.zeros_like(blk)
    return jnp.where(lane < HD, blk, zero), jnp.where(lane >= HD, blk, zero)


def column(row):
    return jnp.transpose(jnp.broadcast_to(row, (128, row.shape[1])))


def pack_kernel(pairs, qkv_ref, cot_ref, out_ref):
    for p in range(pairs):
        for e in range(2):
            col = p * 384 + e * 192
            out_ref[e, p] = jnp.concatenate(
                [
                    qkv_ref[:, col : col + 64],
                    cot_ref[:, p * 128 + e * 64 : p * 128 + e * 64 + 64],
                    qkv_ref[:, col + 64 : col + 192],
                ],
                axis=1,
            )


def pack_call(qkv, cot):
    rows = qkv.shape[0]
    pairs = 4
    steps = qkv.shape[1] // (384 * pairs)
    return pl.pallas_call(
        functools.partial(pack_kernel, pairs),
        grid=(steps,),
        in_specs=[
            pl.BlockSpec((rows, 384 * pairs), lambda i: (0, i)),
            pl.BlockSpec((rows, 128 * pairs), lambda i: (0, i)),
        ],
        out_specs=pl.BlockSpec((2, pairs, rows, 256), lambda i: (0, i, 0, 0)),
        out_shape=jax.ShapeDtypeStruct((2, steps * pairs, rows, 256), bf16),
        compiler_params=params(),
        cost_estimate=cost(0, 4 * qkv.size),
        name="pack_heads",
    )(qkv, cot)


def scores_kernel(first, kt, unroll, sc_ref, qd_ref, kv_ref, e_ref, dp_ref, st_ref, s_scr, m_scr):
    i = pl.program_id(0)
    count = pl.num_programs(0)
    keys = kv_ref.shape[0]
    total = qd_ref.shape[0] // QB

    def block(j):
        at = lax.rem(first + j + sc_ref[0], total)
        return halves(qd_ref[pl.ds(pl.multiple_of(at * QB, QB), QB), :])

    def scores(t, q, mx):
        rows = pl.ds(pl.multiple_of(t * kt, kt), kt)
        s = dot(kv_ref[rows, :], q, 1, 1)
        s_scr[rows, :] = s
        return jnp.maximum(mx, fold8(s, jnp.max))

    neg = jnp.full((8, QB), -jnp.inf, f32)

    @pl.when(i == 0)
    def _():
        q = block(0)[0]
        m_scr[...] = lax.fori_loop(
            0, keys // kt, lambda t, mx: scores(t, q, mx), neg, unroll=4
        )

    m = jnp.max(m_scr[...], axis=0, keepdims=True)
    d = block(i)[1]
    q_next = block(jnp.minimum(i + 1, count - 1))[0]

    def step(t, carry):
        mx, l, acc = carry
        rows = pl.ds(pl.multiple_of(t * kt, kt), kt)
        e = jnp.exp2((s_scr[rows, :] - m) * LOG2E_SCALED)
        dp = dot(kv_ref[rows, :], d, 1, 1).astype(bf16)
        e_ref[0, rows, :] = e.astype(bf16)
        dp_ref[0, rows, :] = dp
        l = l + fold8(e, jnp.sum)
        acc = acc + fold8(e * dp.astype(f32), jnp.sum)
        mx = scores(t, q_next, mx)
        return mx, l, acc

    z = jnp.zeros((8, QB), f32)
    mx, l, acc = lax.fori_loop(0, keys // kt, step, (neg, z, z), unroll=unroll)
    m_scr[...] = mx
    row = lax.broadcasted_iota(jnp.int32, (8, QB), 0)
    st_ref[...] = jnp.where(
        row == 0,
        m,
        jnp.where(
            row == 1, jnp.sum(l, axis=0, keepdims=True), jnp.sum(acc, axis=0, keepdims=True)
        ),
    )


def scores_call(sc, joint, first, blocks):
    tokens = joint.shape[0]
    kt = 256
    big = jax.ShapeDtypeStruct((blocks, tokens, QB), bf16)
    return pl.pallas_call(
        functools.partial(scores_kernel, first, kt, tokens // kt),
        grid_spec=pltpu.PrefetchScalarGridSpec(
            num_scalar_prefetch=1,
            grid=(blocks,),
            in_specs=[
                pl.BlockSpec((tokens, 128), lambda i, sc: (0, 0)),
                pl.BlockSpec((tokens, 128), lambda i, sc: (0, 1)),
            ],
            out_specs=[
                pl.BlockSpec((1, tokens, QB), lambda i, sc: (i, 0, 0)),
                pl.BlockSpec((1, tokens, QB), lambda i, sc: (i, 0, 0)),
                pl.BlockSpec((8, QB), lambda i, sc: (0, i)),
            ],
            scratch_shapes=[pltpu.VMEM((tokens, QB), f32), pltpu.VMEM((8, QB), f32)],
        ),
        out_shape=[big, big, jax.ShapeDtypeStruct((8, blocks * QB), f32)],
        compiler_params=params(),
        cost_estimate=cost(8 * blocks * QB * tokens * 128, 4 * blocks * tokens * QB),
        name="image_scores",
    )(sc, joint, joint)


def text_query_kernel(
    sc_ref, joint_ref, text_ref, dkv_ref, dkvt_ref, dqt_ref, s_scr, e_scr, dp_scr
):
    keys = joint_ref.shape[0]
    kt = 256
    tiles = keys // kt
    q, d = halves(text_ref[:, 0:128])
    text_kv = text_ref[:, 128:256]

    def rows_of(t):
        return pl.ds(pl.multiple_of(t * kt, kt), kt)

    def scores(t, mx):
        s = dot(joint_ref[rows_of(t), 128:256], q, 1, 1)
        s_scr[rows_of(t), :] = s
        return jnp.maximum(mx, fold8(s, jnp.max))

    neg = jnp.full((8, QB), -jnp.inf, f32)
    mx = lax.fori_loop(0, tiles, scores, neg, unroll=4)
    key = lax.broadcasted_iota(jnp.int32, (kt, QB), 0)
    st = jnp.where(key < sc_ref[1], dot(text_kv, q, 1, 1), jnp.float32(-1e30))
    m = jnp.max(jnp.maximum(mx, fold8(st, jnp.max)), axis=0, keepdims=True)

    def weigh(s, kv, carry):
        l, acc = carry
        e = jnp.exp2((s - m) * LOG2E_SCALED)
        dp = dot(kv, d, 1, 1).astype(bf16)
        l = l + fold8(e, jnp.sum)
        acc = acc + fold8(e * dp.astype(f32), jnp.sum)
        return e.astype(bf16), dp, (l, acc)

    def second(t, carry):
        e, dp, carry = weigh(s_scr[rows_of(t), :], joint_ref[rows_of(t), 128:256], carry)
        e_scr[rows_of(t), :] = e
        dp_scr[rows_of(t), :] = dp
        return carry

    z = jnp.zeros((8, QB), f32)
    carry = lax.fori_loop(0, tiles, second, (z, z), unroll=4)
    et, dpt, (l, acc) = weigh(st, text_kv, carry)
    r = 1.0 / jnp.sum(l, axis=0, keepdims=True)
    delta = jnp.sum(acc, axis=0, keepdims=True) * r
    r8 = r * 0.125
    qw = (q.astype(f32) * column(r8)).astype(bf16)
    dw = (d.astype(f32) * column(r)).astype(bf16)

    def third(e, dp, kv):
        ds = (e.astype(f32) * (dp.astype(f32) - delta)).astype(bf16)
        k_t = jnp.transpose(kv.astype(f32))[0:HD, :].astype(bf16)
        return dot(e, dw, 1, 0) + dot(ds, qw, 1, 0), dot(k_t, ds, 1, 0)

    dkvt, dq = third(et, dpt, text_kv)
    dkvt_ref[...] = dkvt

    def last(t, dq):
        dkv, more = third(e_scr[rows_of(t), :], dp_scr[rows_of(t), :], joint_ref[rows_of(t), 128:256])
        dkv_ref[rows_of(t), :] = dkv
        return dq + more

    dq = lax.fori_loop(0, tiles, last, dq, unroll=2)
    dqt_ref[...] = dq * r8


def text_query_call(sc, joint, text):
    tokens = joint.shape[0]
    rows = text.shape[0]
    shapes = [(tokens, 128), (rows, 128), (HD, rows)]
    return pl.pallas_call(
        text_query_kernel,
        grid_spec=pltpu.PrefetchScalarGridSpec(
            num_scalar_prefetch=1,
            grid=(1,),
            in_specs=[full_spec(joint.shape), full_spec(text.shape)],
            out_specs=[full_spec(s) for s in shapes],
            scratch_shapes=[
                pltpu.VMEM((tokens, QB), f32),
                pltpu.VMEM((tokens, QB), bf16),
                pltpu.VMEM((tokens, QB), bf16),
            ],
        ),
        out_shape=[jax.ShapeDtypeStruct(s, f32) for s in shapes],
        compiler_params=params(),
        cost_estimate=cost(16 * rows * tokens * 128, 8 * tokens * 128),
        name="text_queries",
    )(sc, joint, text)


def text_key_kernel(
    sc_ref, qd_ref, text_ref, st_ref, dkvt_ref, dqtx_ref, qdw_ref, row_ref, dq_ref, gt_ref, acc
):
    i = pl.program_id(0)

    @pl.when(i == 0)
    def _():
        acc[...] = dkvt_ref[...]

    q, d = halves(qd_ref[...])
    kv = text_ref[:, 128:256]
    key = lax.broadcasted_iota(jnp.int32, (kv.shape[0], QB), 0)
    s = jnp.where(key < sc_ref[1], dot(kv, q, 1, 1), jnp.float32(-1e30))
    m_img, l_img, d_img = st_ref[0:1, :], st_ref[1:2, :], st_ref[2:3, :]
    m = jnp.maximum(m_img, jnp.max(s, axis=0, keepdims=True))
    a = jnp.exp2((m_img - m) * LOG2E_SCALED)
    e = jnp.exp2((s - m) * LOG2E_SCALED)
    dp = dot(kv, d, 1, 1).astype(bf16).astype(f32)
    r = 1.0 / (a * l_img + jnp.sum(e, axis=0, keepdims=True))
    delta = (a * d_img + jnp.sum(e * dp, axis=0, keepdims=True)) * r
    w = a * r
    ds = (e * (dp - delta)).astype(bf16)
    rc, wc = column(r), column(w)
    qf, df = q.astype(f32), d.astype(f32)
    qdw_ref[...] = ((qf * 0.125 + df) * wc).astype(bf16)
    acc[...] += dot(e.astype(bf16), (df * rc).astype(bf16), 1, 0) + dot(
        ds, (qf * (rc * 0.125)).astype(bf16), 1, 0
    )
    k_t = jnp.transpose(kv.astype(f32))[0:HD, :].astype(bf16)
    dq_ref[...] = dot(k_t, ds, 1, 0) * (r * 0.125)
    row = lax.broadcasted_iota(jnp.int32, (8, QB), 0)
    row_ref[...] = jnp.where(row == 0, delta, w * 0.125)

    @pl.when(i == pl.num_programs(0) - 1)
    def _():
        gt_ref[0:HD, :] = dqtx_ref[...].astype(bf16)
        gt_ref[HD : 3 * HD, :] = jnp.transpose(acc[...]).astype(bf16)


def text_key_call(sc, joint, text, stats, dkvt, dqtx):
    tokens = joint.shape[0]
    rows = text.shape[0]
    blocks = tokens // QB
    return pl.pallas_call(
        text_key_kernel,
        grid_spec=pltpu.PrefetchScalarGridSpec(
            num_scalar_prefetch=1,
            grid=(blocks,),
            in_specs=[
                pl.BlockSpec((QB, 128), lambda i, sc: (lax.rem(i + sc[0], blocks), 0)),
                full_spec(text.shape),
                pl.BlockSpec((8, QB), lambda i, sc: (0, i)),
                full_spec(dkvt.shape),
                full_spec(dqtx.shape),
            ],
            out_specs=[
                pl.BlockSpec((QB, 128), lambda i, sc: (i, 0)),
                pl.BlockSpec((8, QB), lambda i, sc: (0, i)),
                pl.BlockSpec((HD, QB), lambda i, sc: (0, i)),
                full_spec((3 * HD, rows)),
            ],
            scratch_shapes=[pltpu.VMEM((rows, 128), f32)],
        ),
        out_shape=[
            jax.ShapeDtypeStruct((tokens, 128), bf16),
            jax.ShapeDtypeStruct((8, tokens), f32),
            jax.ShapeDtypeStruct((HD, tokens), f32),
            jax.ShapeDtypeStruct((3 * HD, rows), bf16),
        ],
        compiler_params=params(),
        cost_estimate=cost(16 * rows * tokens * 128, 8 * tokens * 128),
        name="text_keys",
    )(sc, joint, text, stats, dkvt, dqtx)


def grads_kernel(blocks, done, *refs):
    sc_ref, e_ref, dp_ref, qdw_ref, row_ref, kv_ref, dkv_in = refs[:7]
    if done:
        dq_in, dq_text, dkv_ref, dq_ref, acc = refs[7:]
    else:
        dkv_ref, acc = refs[7:]
        dq_ref = acc
    i = pl.program_id(0)
    k_t = jnp.transpose(kv_ref[...].astype(f32))[0:HD, :].astype(bf16)
    dkv = dkv_in[...]

    @pl.when(i == 0)
    def _():
        acc[...] = dq_in[...] if done else jnp.zeros_like(acc)

    for j in range(blocks):
        c = slice(j * QB, (j + 1) * QB)
        e = e_ref[j]
        ds = (e.astype(f32) * (dp_ref[j].astype(f32) - row_ref[0:1, c])).astype(bf16)
        q, d = halves(qdw_ref[c, :])
        dkv = dkv + dot(e, d, 1, 0) + dot(ds, q, 1, 0)
        acc[:, c] += dot(k_t, ds, 1, 0)
    dkv_ref[...] = dkv.astype(dkv_ref.dtype)
    if done:

        @pl.when(i == pl.num_programs(0) - 1)
        def _():
            dq_ref[...] = (acc[...] * row_ref[1:2, :] + dq_text[...]).astype(bf16)


def grads_call(sc, e, dp, qdw, row, joint, dkv_in, dq_in, dq_text, half, own_keys):
    blocks, tokens, _ = e.shape
    key_blocks = blocks
    queries = blocks * QB
    done = dq_in is not None
    whole = dkv_in.shape[0] == tokens
    all_blocks = tokens // QB

    def key_at(i, sc):
        return lax.rem(i + (key_blocks if own_keys else 0) + sc[0], all_blocks)

    in_specs = [
        pl.BlockSpec((blocks, QB, QB), lambda i, sc: (0, key_at(i, sc), 0)),
        pl.BlockSpec((blocks, QB, QB), lambda i, sc: (0, key_at(i, sc), 0)),
        pl.BlockSpec((queries, 128), lambda i, sc: (half, 0)),
        pl.BlockSpec((8, queries), lambda i, sc: (0, half)),
        pl.BlockSpec((QB, 128), lambda i, sc: (key_at(i, sc), 1)),
        pl.BlockSpec((QB, 128), lambda i, sc: (key_at(i, sc) if whole else i, 0)),
    ]
    args = [e, dp, qdw, row, joint, dkv_in]
    last_dkv = not whole
    out_specs = [pl.BlockSpec((QB, 128), lambda i, sc: (i, 0))]
    out_shape = [jax.ShapeDtypeStruct((key_blocks * QB, 128), bf16 if last_dkv else f32)]
    dq_shape = (HD, queries)
    scratch = []
    if done:
        in_specs += [full_spec(dq_shape), pl.BlockSpec(dq_shape, lambda i, sc: (0, half))]
        args += [dq_in, dq_text]
        out_shape.append(jax.ShapeDtypeStruct(dq_shape, bf16))
        scratch = [pltpu.VMEM(dq_shape, f32)]
    else:
        out_shape.append(jax.ShapeDtypeStruct(dq_shape, f32))
    out_specs.append(full_spec(dq_shape))
    return pl.pallas_call(
        functools.partial(grads_kernel, blocks, done),
        grid_spec=pltpu.PrefetchScalarGridSpec(
            num_scalar_prefetch=1,
            grid=(key_blocks,),
            in_specs=in_specs,
            out_specs=out_specs,
            scratch_shapes=scratch,
        ),
        out_shape=out_shape,
        compiler_params=params(),
        cost_estimate=cost(
            12 * queries * key_blocks * QB * 128, 4 * queries * key_blocks * QB
        ),
        name="image_grads",
    )(sc, *args)


def project_kernel(sc_ref, tf_ref, w_ref, cot_ref, own_ref, other_ref):
    qkv = dot(tf_ref[...], w_ref[...], 1, 0).astype(bf16)
    heads = []
    for e in range(2):
        heads.append(
            jnp.concatenate(
                [
                    qkv[:, e * 192 : e * 192 + 64],
                    cot_ref[:, e * 64 : e * 64 + 64],
                    qkv[:, e * 192 + 64 : e * 192 + 192],
                ],
                axis=1,
            )
        )
    flag = jnp.zeros(heads[0].shape, jnp.int32) + sc_ref[2]
    own_ref[...] = jnp.where(flag == 0, heads[0], heads[1])
    other_ref[...] = jnp.where(flag == 0, heads[1], heads[0])


def project_call(sc, tf, w, cot):
    rows = tf.shape[0]
    out = jax.ShapeDtypeStruct((rows, 256), bf16)
    return pl.pallas_call(
        project_kernel,
        grid_spec=pltpu.PrefetchScalarGridSpec(
            num_scalar_prefetch=1,
            grid=(1,),
            in_specs=[full_spec(tf.shape), full_spec(w.shape), full_spec(cot.shape)],
            out_specs=[full_spec(out.shape)] * 2,
        ),
        out_shape=[out, out],
        compiler_params=params(),
        cost_estimate=cost(2 * tf.size * w.shape[1], 2 * w.size),
        name="text_projection",
    )(sc, tf, w, cot)


def join_kernel(sc_ref, dq_ref, dkv_ref, dq_got, dkv_got, out_ref):
    def rows(dq, dkv):
        return jnp.concatenate([jnp.transpose(dq[...].astype(f32)).astype(bf16), dkv[...]], axis=1)

    own, got = rows(dq_ref, dkv_ref), rows(dq_got, dkv_got)

    @pl.when(sc_ref[2] == 0)
    def _():
        out_ref[...] = jnp.concatenate([own, got], axis=1)

    @pl.when(sc_ref[2] != 0)
    def _():
        out_ref[...] = jnp.concatenate([got, own], axis=1)


def join_call(sc, dq, dkv, dq_got, dkv_got):
    tokens = dkv.shape[0]
    dq_spec = pl.BlockSpec((HD, 512), lambda i, sc: (0, i))
    dkv_spec = pl.BlockSpec((512, 128), lambda i, sc: (i, 0))
    return pl.pallas_call(
        join_kernel,
        grid_spec=pltpu.PrefetchScalarGridSpec(
            num_scalar_prefetch=1,
            grid=(tokens // 512,),
            in_specs=[dq_spec, dkv_spec, dq_spec, dkv_spec],
            out_specs=pl.BlockSpec((512, 384), lambda i, sc: (i, 0)),
        ),
        out_shape=jax.ShapeDtypeStruct((tokens, 384), bf16),
        compiler_params=params(),
        cost_estimate=cost(0, 4 * tokens * 384),
        name="join_heads",
    )(sc, dq, dkv, dq_got, dkv_got)


def proj_grad_kernel(tf_ref, gt_ref, out_ref):
    groups, samples = tf_ref.shape[0], tf_ref.shape[1]
    rows = tf_ref.shape[2]
    for h in range(groups):
        total = None
        for b in range(samples):
            for p in range(groups):
                term = dot(tf_ref[p, b], gt_ref[h, b, :, p * rows : (p + 1) * rows], 0, 1)
                total = term if total is None else total + term
        out_ref[:, h * 192 : (h + 1) * 192] = total


def proj_grad_call(tf, gt):
    out = jax.ShapeDtypeStruct((tf.shape[3], 384), f32)
    return pl.pallas_call(
        proj_grad_kernel,
        grid=(1,),
        in_specs=[full_spec(tf.shape), full_spec(gt.shape)],
        out_specs=full_spec(out.shape),
        out_shape=out,
        compiler_params=params(),
        cost_estimate=cost(2 * tf.size * 384, 2 * (tf.size + gt.size)),
        name="projection_grad",
    )(tf, gt)


def rms_norm(values_in, norm_scale):
    mean_sq = jnp.mean(values_in * values_in, axis=-1, keepdims=True)
    return values_in * lax.rsqrt(mean_sq + 1e-06) * norm_scale


def on_device(
    text_states,
    text_lengths,
    norm_gain,
    final_gain,
    wi_gate,
    wi_up,
    wo_weight,
    text_proj,
    image_qkv,
    image_cot,
    text_cot,
    groups,
    slots,
    samples,
):
    grp = lax.axis_index("grp")
    slot = lax.axis_index("seq")
    half_tokens = image_qkv.shape[1] * slots
    half_blocks = half_tokens // QB
    blocks = groups * half_blocks
    flip = [(0, 1), (1, 0)]
    sc = jnp.stack(
        [(1 - grp) * half_blocks, text_lengths[0], grp, jnp.int32(0)]
    ).astype(jnp.int32)

    packed = pack_call(image_qkv[0], image_cot[0])
    packed = packed.reshape(groups * slots, image_qkv.shape[1], 256)
    joint = lax.all_to_all(packed, ("grp", "seq"), 0, 0, tiled=True)
    joint = joint.reshape(groups * half_tokens, 256)

    states = text_states[0]
    normed = rms_norm(states.astype(f32), norm_gain).astype(bf16)
    gate_act = jnp.dot(normed, wi_gate, preferred_element_type=f32)
    up_act = jnp.dot(normed, wi_up, preferred_element_type=f32)
    hidden = (jax.nn.gelu(gate_act, approximate=True) * up_act).astype(bf16)
    ffn = jnp.dot(hidden, wo_weight, preferred_element_type=f32).astype(bf16)
    rows, width = states.shape
    few = rows // slots
    terms = lax.all_to_all(ffn.reshape(slots, few, width), "seq", 0, 0, tiled=True)
    mine = lax.dynamic_slice_in_dim(states, slot * few, few, axis=0).astype(f32)
    encoded = mine + jnp.sum(terms.astype(f32), axis=0)
    final_rows = rms_norm(encoded, final_gain).astype(bf16)
    spread = jnp.broadcast_to(final_rows[None], (slots, few, width))
    text_final = lax.all_to_all(spread, "seq", 0, 0, tiled=True).reshape(rows, width)

    e_a, dp_a, st_a = scores_call(sc, joint, 0, half_blocks)
    e_b, dp_b, st_b = scores_call(sc, joint, half_blocks, half_blocks)

    own, other = project_call(sc, text_final, text_proj, text_cot[0])
    got = lax.ppermute(other, "grp", flip)
    text = jnp.where(
        grp == 0, jnp.concatenate([own, got], axis=0), jnp.concatenate([got, own], axis=0)
    )
    features = jnp.moveaxis(
        text_final.reshape(rows, groups * samples, width // (groups * samples)), 1, 0
    )
    features = lax.all_to_all(features, ("grp", "dp"), 0, 0, tiled=True)

    dkv0, dkvt, dqtx = text_query_call(sc, joint, text)
    stats = jnp.concatenate([st_a, st_b], axis=1)
    qdw, row, dq_text, gt = text_key_call(sc, joint, text, stats, dkvt, dqtx)
    gt_all = lax.all_gather(gt, ("grp", "dp"))

    dkv1, dq_a = grads_call(sc, e_a, dp_a, qdw, row, joint, dkv0, None, None, 0, False)
    dkv_other, dq_b = grads_call(sc, e_b, dp_b, qdw, row, joint, dkv1, None, None, 1, False)
    dkv_got = lax.ppermute(dkv_other, "grp", flip)
    dkv2, dq_other = grads_call(sc, e_a, dp_a, qdw, row, joint, dkv0, dq_a, dq_text, 0, True)
    dq_got = lax.ppermute(dq_other, "grp", flip)
    dkv_own, dq_own = grads_call(sc, e_b, dp_b, qdw, row, joint, dkv2, dq_b, dq_text, 1, True)
    image_out = join_call(sc, dq_own, dkv_own, dq_got, dkv_got)[None]

    proj_grad = proj_grad_call(
        features.reshape(groups, samples, rows, width // (groups * samples)),
        gt_all.reshape((groups, samples) + gt.shape),
    )
    return (image_out, proj_grad)


def solution(mesh):
    placed = (
        P("dp", "grp", None),
        P("dp"),
        P(),
        P(),
        P(None, "seq"),
        P(None, "seq"),
        P("seq", None),
        P(None, "seq"),
        P("dp", ("grp", "seq"), None),
        P("dp", ("grp", "seq"), None),
        P("dp", "grp", "seq"),
    )
    step = functools.partial(
        on_device,
        groups=mesh.shape["grp"],
        slots=mesh.shape["seq"],
        samples=mesh.shape["dp"],
    )
    return jax.shard_map(
        step,
        mesh=mesh,
        in_specs=placed,
        out_specs=(P("dp", "grp", "seq"), P(("grp", "dp"), "seq")),
        check_vma=False,
    )
```

```python
import functools

import jax
import jax.numpy as jnp
from jax import lax
from jax.experimental import pallas as pl
from jax.experimental.pallas import tpu as pltpu
from jax.sharding import PartitionSpec as P

f32, bf16 = jnp.float32, jnp.bfloat16
HD = 64
QB = 256
WIDE = 4
LOG2E_SCALED = 1.4426950408889634 / 8.0
VMEM_LIMIT = 50 << 20


def dot(a, b, ca, cb):
    return lax.dot_general(a, b, (((ca,), (cb,)), ((), ())), preferred_element_type=f32)


def fold8(x, op):
    return op(x.reshape(x.shape[0] // 8, 8, x.shape[1]), axis=0)


def params(limit=VMEM_LIMIT):
    return pltpu.CompilerParams(vmem_limit_bytes=limit)


def cost(flops, nbytes, trans=0):
    return pl.CostEstimate(flops=int(flops), bytes_accessed=int(nbytes), transcendentals=int(trans))


def full_spec(shape):
    return pl.BlockSpec(shape, lambda i, *_: (0,) * len(shape))


def halves(blk):
    lane = lax.broadcasted_iota(jnp.int32, blk.shape, 1)
    zero = jnp.zeros_like(blk)
    return jnp.where(lane < HD, blk, zero), jnp.where(lane >= HD, blk, zero)


def column(row):
    return jnp.transpose(jnp.broadcast_to(row, (128, row.shape[1])))


def pack_kernel(pairs, qkv_ref, cot_ref, out_ref):
    for p in range(pairs):
        for e in range(2):
            col = p * 384 + e * 192
            out_ref[e, p] = jnp.concatenate(
                [
                    qkv_ref[:, col : col + 64],
                    cot_ref[:, p * 128 + e * 64 : p * 128 + e * 64 + 64],
                    qkv_ref[:, col + 64 : col + 192],
                ],
                axis=1,
            )


def pack_call(qkv, cot):
    rows = qkv.shape[0]
    pairs = 4
    steps = qkv.shape[1] // (384 * pairs)
    return pl.pallas_call(
        functools.partial(pack_kernel, pairs),
        grid=(steps,),
        in_specs=[
            pl.BlockSpec((rows, 384 * pairs), lambda i: (0, i)),
            pl.BlockSpec((rows, 128 * pairs), lambda i: (0, i)),
        ],
        out_specs=pl.BlockSpec((2, pairs, rows, 256), lambda i: (0, i, 0, 0)),
        out_shape=jax.ShapeDtypeStruct((2, steps * pairs, rows, 256), bf16),
        compiler_params=params(),
        cost_estimate=cost(0, 4 * qkv.size),
        name="pack_heads",
    )(qkv, cot)


def scores_kernel(first, kt, unroll, sc_ref, qd_ref, kv_ref, e_ref, dp_ref, st_ref, s_scr, m_scr):
    i = pl.program_id(0)
    count = pl.num_programs(0)
    keys = kv_ref.shape[0]
    total = qd_ref.shape[0] // QB

    def block(j):
        at = lax.rem(first + j + sc_ref[0], total)
        return halves(qd_ref[pl.ds(pl.multiple_of(at * QB, QB), QB), :])

    def scores(t, q, mx):
        rows = pl.ds(pl.multiple_of(t * kt, kt), kt)
        s = dot(kv_ref[rows, :], q, 1, 1)
        s_scr[rows, :] = s
        return jnp.maximum(mx, fold8(s, jnp.max))

    neg = jnp.full((8, QB), -jnp.inf, f32)

    @pl.when(i == 0)
    def _():
        q = block(0)[0]
        m_scr[...] = lax.fori_loop(
            0, keys // kt, lambda t, mx: scores(t, q, mx), neg, unroll=4
        )

    m = jnp.max(m_scr[...], axis=0, keepdims=True)
    d = block(i)[1]
    q_next = block(jnp.minimum(i + 1, count - 1))[0]

    def step(t, carry):
        mx, l, acc = carry
        rows = pl.ds(pl.multiple_of(t * kt, kt), kt)
        e = jnp.exp2((s_scr[rows, :] - m) * LOG2E_SCALED)
        dp = dot(kv_ref[rows, :], d, 1, 1).astype(bf16)
        e_ref[0, rows, :] = e.astype(bf16)
        dp_ref[0, rows, :] = dp
        l = l + fold8(e, jnp.sum)
        acc = acc + fold8(e * dp.astype(f32), jnp.sum)
        mx = scores(t, q_next, mx)
        return mx, l, acc

    z = jnp.zeros((8, QB), f32)
    mx, l, acc = lax.fori_loop(0, keys // kt, step, (neg, z, z), unroll=unroll)
    m_scr[...] = mx
    row = lax.broadcasted_iota(jnp.int32, (8, QB), 0)
    st_ref[...] = jnp.where(
        row == 0,
        m,
        jnp.where(
            row == 1, jnp.sum(l, axis=0, keepdims=True), jnp.sum(acc, axis=0, keepdims=True)
        ),
    )


def scores_call(sc, joint, first, blocks):
    tokens = joint.shape[0]
    kt = 256
    big = jax.ShapeDtypeStruct((blocks, tokens, QB), bf16)
    return pl.pallas_call(
        functools.partial(scores_kernel, first, kt, tokens // kt),
        grid_spec=pltpu.PrefetchScalarGridSpec(
            num_scalar_prefetch=1,
            grid=(blocks,),
            in_specs=[
                pl.BlockSpec((tokens, 128), lambda i, sc: (0, 0)),
                pl.BlockSpec((tokens, 128), lambda i, sc: (0, 1)),
            ],
            out_specs=[
                pl.BlockSpec((1, tokens, QB), lambda i, sc: (i, 0, 0)),
                pl.BlockSpec((1, tokens, QB), lambda i, sc: (i, 0, 0)),
                pl.BlockSpec((8, QB), lambda i, sc: (0, i)),
            ],
            scratch_shapes=[pltpu.VMEM((tokens, QB), f32), pltpu.VMEM((8, QB), f32)],
        ),
        out_shape=[big, big, jax.ShapeDtypeStruct((8, blocks * QB), f32)],
        compiler_params=params(),
        cost_estimate=cost(8 * blocks * QB * tokens * 128, 4 * blocks * tokens * QB),
        name="image_scores",
    )(sc, joint, joint)


def text_query_kernel(
    sc_ref, joint_ref, text_ref, dkv_ref, dkvt_ref, dqt_ref, s_scr, e_scr, dp_scr
):
    keys = joint_ref.shape[0]
    kt = 256
    tiles = keys // kt
    q, d = halves(text_ref[:, 0:128])
    text_kv = text_ref[:, 128:256]

    def rows_of(t):
        return pl.ds(pl.multiple_of(t * kt, kt), kt)

    def scores(t, mx):
        s = dot(joint_ref[rows_of(t), 128:256], q, 1, 1)
        s_scr[rows_of(t), :] = s
        return jnp.maximum(mx, fold8(s, jnp.max))

    neg = jnp.full((8, QB), -jnp.inf, f32)
    mx = lax.fori_loop(0, tiles, scores, neg, unroll=tiles)
    key = lax.broadcasted_iota(jnp.int32, (kt, QB), 0)
    st = jnp.where(key < sc_ref[1], dot(text_kv, q, 1, 1), jnp.float32(-1e30))
    m = jnp.max(jnp.maximum(mx, fold8(st, jnp.max)), axis=0, keepdims=True)

    def weigh(s, kv, carry):
        l, acc = carry
        e = jnp.exp2((s - m) * LOG2E_SCALED)
        dp = dot(kv, d, 1, 1).astype(bf16)
        l = l + fold8(e, jnp.sum)
        acc = acc + fold8(e * dp.astype(f32), jnp.sum)
        return e.astype(bf16), dp, (l, acc)

    def second(t, carry):
        e, dp, carry = weigh(s_scr[rows_of(t), :], joint_ref[rows_of(t), 128:256], carry)
        e_scr[rows_of(t), :] = e
        dp_scr[rows_of(t), :] = dp
        return carry

    z = jnp.zeros((8, QB), f32)
    carry = lax.fori_loop(0, tiles, second, (z, z), unroll=tiles)
    et, dpt, (l, acc) = weigh(st, text_kv, carry)
    r = 1.0 / jnp.sum(l, axis=0, keepdims=True)
    delta = jnp.sum(acc, axis=0, keepdims=True) * r
    r8 = r * 0.125
    qw = (q.astype(f32) * column(r8)).astype(bf16)
    dw = (d.astype(f32) * column(r)).astype(bf16)

    def third(e, dp, kv):
        ds = (e.astype(f32) * (dp.astype(f32) - delta)).astype(bf16)
        k_t = jnp.transpose(kv.astype(f32))[0:HD, :].astype(bf16)
        return dot(e, dw, 1, 0) + dot(ds, qw, 1, 0), dot(k_t, ds, 1, 0)

    dkvt, dq = third(et, dpt, text_kv)
    dkvt_ref[...] = dkvt

    def last(t, dq):
        dkv, more = third(e_scr[rows_of(t), :], dp_scr[rows_of(t), :], joint_ref[rows_of(t), 128:256])
        dkv_ref[rows_of(t), :] = dkv
        return dq + more

    dq = lax.fori_loop(0, tiles, last, dq, unroll=tiles)
    dqt_ref[...] = dq * r8


def text_query_call(sc, joint, text):
    tokens = joint.shape[0]
    rows = text.shape[0]
    shapes = [(tokens, 128), (rows, 128), (HD, rows)]
    return pl.pallas_call(
        text_query_kernel,
        grid_spec=pltpu.PrefetchScalarGridSpec(
            num_scalar_prefetch=1,
            grid=(1,),
            in_specs=[full_spec(joint.shape), full_spec(text.shape)],
            out_specs=[full_spec(s) for s in shapes],
            scratch_shapes=[
                pltpu.VMEM((tokens, QB), f32),
                pltpu.VMEM((tokens, QB), bf16),
                pltpu.VMEM((tokens, QB), bf16),
            ],
        ),
        out_shape=[jax.ShapeDtypeStruct(s, f32) for s in shapes],
        compiler_params=params(),
        cost_estimate=cost(16 * rows * tokens * 128, 8 * tokens * 128),
        name="text_queries",
    )(sc, joint, text)


def text_key_kernel(
    sc_ref, qd_ref, text_ref, st_ref, dkvt_ref, dqtx_ref, qdw_ref, row_ref, dq_ref, gt_ref, acc
):
    i = pl.program_id(0)
    wide = qd_ref.shape[0]

    @pl.when(i == 0)
    def _():
        acc[...] = dkvt_ref[...]

    q, d = halves(qd_ref[...])
    kv = text_ref[:, 128:256]
    key = lax.broadcasted_iota(jnp.int32, (kv.shape[0], wide), 0)
    s = jnp.where(key < sc_ref[1], dot(kv, q, 1, 1), jnp.float32(-1e30))
    m_img, l_img, d_img = st_ref[0:1, :], st_ref[1:2, :], st_ref[2:3, :]
    m = jnp.maximum(m_img, jnp.max(s, axis=0, keepdims=True))
    a = jnp.exp2((m_img - m) * LOG2E_SCALED)
    e = jnp.exp2((s - m) * LOG2E_SCALED)
    dp = dot(kv, d, 1, 1).astype(bf16).astype(f32)
    r = 1.0 / (a * l_img + jnp.sum(e, axis=0, keepdims=True))
    delta = (a * d_img + jnp.sum(e * dp, axis=0, keepdims=True)) * r
    w = a * r
    ds = (e * (dp - delta)).astype(bf16)
    rc, wc = column(r), column(w)
    qdf = q.astype(f32) * 0.125 + d.astype(f32)
    qdw_ref[...] = (qdf * wc).astype(bf16)
    qr, dr = halves((qdf * rc).astype(bf16))
    acc[...] += dot(e.astype(bf16), dr, 1, 0) + dot(ds, qr, 1, 0)
    k_t = jnp.transpose(kv.astype(f32))[0:HD, :].astype(bf16)
    dq_ref[...] = dot(k_t, ds, 1, 0) * (r * 0.125)
    row = lax.broadcasted_iota(jnp.int32, (8, wide), 0)
    row_ref[...] = jnp.where(row == 0, delta, w * 0.125)

    @pl.when(i == pl.num_programs(0) - 1)
    def _():
        gt_ref[0:HD, :] = dqtx_ref[...].astype(bf16)
        gt_ref[HD : 3 * HD, :] = jnp.transpose(acc[...]).astype(bf16)


def text_key_call(sc, joint, text, stats, dkvt, dqtx):
    tokens = joint.shape[0]
    rows = text.shape[0]
    wide = WIDE * QB
    blocks = tokens // wide
    return pl.pallas_call(
        text_key_kernel,
        grid_spec=pltpu.PrefetchScalarGridSpec(
            num_scalar_prefetch=1,
            grid=(blocks,),
            in_specs=[
                pl.BlockSpec((wide, 128), lambda i, sc: (lax.rem(i + sc[3], blocks), 0)),
                full_spec(text.shape),
                pl.BlockSpec((8, wide), lambda i, sc: (0, i)),
                full_spec(dkvt.shape),
                full_spec(dqtx.shape),
            ],
            out_specs=[
                pl.BlockSpec((wide, 128), lambda i, sc: (i, 0)),
                pl.BlockSpec((8, wide), lambda i, sc: (0, i)),
                pl.BlockSpec((HD, wide), lambda i, sc: (0, i)),
                full_spec((3 * HD, rows)),
            ],
            scratch_shapes=[pltpu.VMEM((rows, 128), f32)],
        ),
        out_shape=[
            jax.ShapeDtypeStruct((tokens, 128), bf16),
            jax.ShapeDtypeStruct((8, tokens), f32),
            jax.ShapeDtypeStruct((HD, tokens), f32),
            jax.ShapeDtypeStruct((3 * HD, rows), bf16),
        ],
        compiler_params=params(),
        cost_estimate=cost(16 * rows * tokens * 128, 8 * tokens * 128),
        name="text_keys",
    )(sc, joint, text, stats, dkvt, dqtx)


def grads_kernel(parts, blocks, done, *refs):
    pairs = refs[1 : 1 + 2 * parts]
    qdw_ref, row_ref, kv_ref, dkv_in = refs[1 + 2 * parts : 5 + 2 * parts]
    rest = refs[5 + 2 * parts :]
    if done:
        dq_in, dq_text, dkv_ref, dq_ref, acc = rest
    else:
        dkv_ref, acc = rest
    i = pl.program_id(0)
    k_t = jnp.transpose(kv_ref[...].astype(f32))[0:HD, :].astype(bf16)
    dkv = dkv_in[...]

    @pl.when(i == 0)
    def _():
        acc[...] = dq_in[...] if done else jnp.zeros_like(acc)

    for n in range(parts * blocks):
        c = slice(n * QB, (n + 1) * QB)
        e = pairs[2 * (n // blocks)][n % blocks]
        dp = pairs[2 * (n // blocks) + 1][n % blocks]
        ds = (e.astype(f32) * (dp.astype(f32) - row_ref[0:1, c])).astype(bf16)
        q, d = halves(qdw_ref[c, :])
        dkv = dkv + dot(e, d, 1, 0) + dot(ds, q, 1, 0)
        acc[:, c] += dot(k_t, ds, 1, 0)
    dkv_ref[...] = dkv.astype(dkv_ref.dtype)
    if done:

        @pl.when(i == pl.num_programs(0) - 1)
        def _():
            dq_ref[...] = (acc[...] * row_ref[1:2, :] + dq_text[...]).astype(bf16)


def grads_call(sc, pairs, qdw, row, joint, dkv_in, dq_in, dq_text, part, own_keys, last):
    blocks, tokens, _ = pairs[0].shape
    parts = len(pairs) // 2
    queries = parts * blocks * QB
    all_blocks = tokens // QB
    key_blocks = all_blocks // 2
    whole = dkv_in.shape[0] == tokens
    done = dq_in is not None

    def key_at(i, sc):
        return lax.rem(i + (key_blocks if own_keys else 0) + sc[0], all_blocks)

    tile = pl.BlockSpec((blocks, QB, QB), lambda i, sc: (0, key_at(i, sc), 0))
    dq_shape = (HD, queries)
    in_specs = [tile] * len(pairs) + [
        pl.BlockSpec((queries, 128), lambda i, sc: (part, 0)),
        pl.BlockSpec((8, queries), lambda i, sc: (0, part)),
        pl.BlockSpec((QB, 128), lambda i, sc: (key_at(i, sc), 1)),
        pl.BlockSpec((QB, 128), lambda i, sc: (key_at(i, sc) if whole else i, 0)),
    ]
    args = list(pairs) + [qdw, row, joint, dkv_in]
    out_shape = [
        jax.ShapeDtypeStruct((key_blocks * QB, 128), bf16 if last else f32),
        jax.ShapeDtypeStruct(dq_shape, bf16 if done else f32),
    ]
    scratch = []
    if done:
        in_specs += [pl.BlockSpec(dq_shape, lambda i, sc: (0, part))] * 2
        args += [dq_in, dq_text]
        scratch = [pltpu.VMEM(dq_shape, f32)]
    return pl.pallas_call(
        functools.partial(grads_kernel, parts, blocks, done),
        grid_spec=pltpu.PrefetchScalarGridSpec(
            num_scalar_prefetch=1,
            grid=(key_blocks,),
            in_specs=in_specs,
            out_specs=[pl.BlockSpec((QB, 128), lambda i, sc: (i, 0)), full_spec(dq_shape)],
            scratch_shapes=scratch,
        ),
        out_shape=out_shape,
        compiler_params=params(),
        cost_estimate=cost(
            12 * queries * key_blocks * QB * 128, 4 * queries * key_blocks * QB
        ),
        name="image_grads",
    )(sc, *args)


def project_kernel(sc_ref, tf_ref, w_ref, cot_ref, own_ref, other_ref):
    qkv = dot(tf_ref[...], w_ref[...], 1, 0).astype(bf16)
    heads = []
    for e in range(2):
        heads.append(
            jnp.concatenate(
                [
                    qkv[:, e * 192 : e * 192 + 64],
                    cot_ref[:, e * 64 : e * 64 + 64],
                    qkv[:, e * 192 + 64 : e * 192 + 192],
                ],
                axis=1,
            )
        )
    flag = jnp.zeros(heads[0].shape, jnp.int32) + sc_ref[2]
    own_ref[...] = jnp.where(flag == 0, heads[0], heads[1])
    other_ref[...] = jnp.where(flag == 0, heads[1], heads[0])


def project_call(sc, tf, w, cot):
    rows = tf.shape[0]
    out = jax.ShapeDtypeStruct((rows, 256), bf16)
    return pl.pallas_call(
        project_kernel,
        grid_spec=pltpu.PrefetchScalarGridSpec(
            num_scalar_prefetch=1,
            grid=(1,),
            in_specs=[full_spec(tf.shape), full_spec(w.shape), full_spec(cot.shape)],
            out_specs=[full_spec(out.shape)] * 2,
        ),
        out_shape=[out, out],
        compiler_params=params(),
        cost_estimate=cost(2 * tf.size * w.shape[1], 2 * w.size),
        name="text_projection",
    )(sc, tf, w, cot)


def join_kernel(sc_ref, dq_ref, dkv_ref, dq_got, dkv_got, out_ref):
    def rows(dq, dkv):
        return jnp.concatenate([jnp.transpose(dq[...].astype(f32)).astype(bf16), dkv[...]], axis=1)

    own, got = rows(dq_ref, dkv_ref), rows(dq_got, dkv_got)

    @pl.when(sc_ref[2] == 0)
    def _():
        out_ref[...] = jnp.concatenate([own, got], axis=1)

    @pl.when(sc_ref[2] != 0)
    def _():
        out_ref[...] = jnp.concatenate([got, own], axis=1)


def join_call(sc, dq, dkv, dq_got, dkv_got):
    tokens = dkv.shape[0]
    dq_spec = pl.BlockSpec((HD, 512), lambda i, sc: (0, i))
    dkv_spec = pl.BlockSpec((512, 128), lambda i, sc: (i, 0))
    return pl.pallas_call(
        join_kernel,
        grid_spec=pltpu.PrefetchScalarGridSpec(
            num_scalar_prefetch=1,
            grid=(tokens // 512,),
            in_specs=[dq_spec, dkv_spec, dq_spec, dkv_spec],
            out_specs=pl.BlockSpec((512, 384), lambda i, sc: (i, 0)),
        ),
        out_shape=jax.ShapeDtypeStruct((tokens, 384), bf16),
        compiler_params=params(),
        cost_estimate=cost(0, 4 * tokens * 384),
        name="join_heads",
    )(sc, dq, dkv, dq_got, dkv_got)


def proj_grad_kernel(rows, all_ref, out_ref):
    groups, samples, _, lanes = all_ref.shape
    parts = out_ref.shape[0] // lanes
    for f in range(parts):
        total = None
        for b in range(samples):
            gt = jnp.concatenate([all_ref[h, b, parts * rows :, :] for h in range(groups)], axis=0)
            for p in range(groups):
                tf = all_ref[p, b, f * rows : (f + 1) * rows, :]
                term = dot(tf, gt[:, p * rows : (p + 1) * rows], 0, 1)
                total = term if total is None else total + term
        out_ref[f * lanes : (f + 1) * lanes, :] = total


def proj_grad_call(everything, rows, width):
    out = jax.ShapeDtypeStruct((width, 384), f32)
    return pl.pallas_call(
        functools.partial(proj_grad_kernel, rows),
        grid=(1,),
        in_specs=[full_spec(everything.shape)],
        out_specs=full_spec(out.shape),
        out_shape=out,
        compiler_params=params(),
        cost_estimate=cost(4 * everything.size * 384, 2 * everything.size),
        name="projection_grad",
    )(everything)


def rms_norm(values_in, norm_scale):
    mean_sq = jnp.mean(values_in * values_in, axis=-1, keepdims=True)
    return values_in * lax.rsqrt(mean_sq + 1e-06) * norm_scale


def on_device(
    text_states,
    text_lengths,
    norm_gain,
    final_gain,
    wi_gate,
    wi_up,
    wo_weight,
    text_proj,
    image_qkv,
    image_cot,
    text_cot,
    groups,
    slots,
    samples,
):
    grp = lax.axis_index("grp")
    slot = lax.axis_index("seq")
    half_tokens = image_qkv.shape[1] * slots
    half_blocks = half_tokens // QB
    blocks = groups * half_blocks
    flip = [(0, 1), (1, 0)]
    sc = jnp.stack(
        [(1 - grp) * half_blocks, text_lengths[0], grp, (1 - grp) * (half_blocks // WIDE)]
    ).astype(jnp.int32)

    packed = pack_call(image_qkv[0], image_cot[0])
    packed = packed.reshape(groups * slots, image_qkv.shape[1], 256)
    joint = lax.all_to_all(packed, ("grp", "seq"), 0, 0, tiled=True)
    joint = joint.reshape(groups * half_tokens, 256)

    states = text_states[0]
    normed = rms_norm(states.astype(f32), norm_gain).astype(bf16)
    gate_act = jnp.dot(normed, wi_gate, preferred_element_type=f32)
    up_act = jnp.dot(normed, wi_up, preferred_element_type=f32)
    hidden = (jax.nn.gelu(gate_act, approximate=True) * up_act).astype(bf16)
    ffn = jnp.dot(hidden, wo_weight, preferred_element_type=f32).astype(bf16)
    rows, width = states.shape
    few = rows // slots
    ffn, joint = lax.optimization_barrier((ffn, joint))
    terms = lax.all_to_all(ffn.reshape(slots, few, width), "seq", 0, 0, tiled=True)
    e_a, dp_a, st_a = scores_call(sc, joint, 0, half_blocks)
    mine = lax.dynamic_slice_in_dim(states, slot * few, few, axis=0).astype(f32)
    encoded = mine + jnp.sum(terms.astype(f32), axis=0)
    final_rows = rms_norm(encoded, final_gain).astype(bf16)
    spread = jnp.broadcast_to(final_rows[None], (slots, few, width))
    spread, joint_b, st_a = lax.optimization_barrier((spread, joint, st_a))
    text_final = lax.all_to_all(spread, "seq", 0, 0, tiled=True).reshape(rows, width)
    e_b, dp_b, st_b = scores_call(sc, joint_b, half_blocks, half_blocks)

    own, other = project_call(sc, text_final, text_proj, text_cot[0])
    got = lax.ppermute(other, "grp", flip)
    text = jnp.where(
        grp == 0, jnp.concatenate([own, got], axis=0), jnp.concatenate([got, own], axis=0)
    )
    dkv0, dkvt, dqtx = text_query_call(sc, joint, text)
    stats = jnp.concatenate([st_a, st_b], axis=1)
    qdw, row, dq_text, gt = text_key_call(sc, joint, text, stats, dkvt, dqtx)

    members = groups * samples
    features = jnp.moveaxis(text_final.reshape(rows, width // 256, 256), 1, 0)
    features = features.reshape(members, width * rows // (256 * members), 256)
    sent = jnp.concatenate([features, jnp.broadcast_to(gt[None], (members,) + gt.shape)], axis=1)
    sent, qdw = lax.optimization_barrier((sent, qdw))
    everything = lax.all_to_all(sent, ("grp", "dp"), 0, 0, tiled=True)

    dkv_other, dq_all = grads_call(
        sc, (e_a, dp_a, e_b, dp_b), qdw, row, joint, dkv0, None, None, 0, False, True
    )
    dkv_got = lax.ppermute(dkv_other, "grp", flip)
    dkv2, dq_other = grads_call(
        sc, (e_a, dp_a), qdw, row, joint, dkv0, dq_all, dq_text, 0, True, False
    )
    dq_got = lax.ppermute(dq_other, "grp", flip)
    dkv_own, dq_own = grads_call(
        sc, (e_b, dp_b), qdw, row, joint, dkv2, dq_all, dq_text, 1, True, True
    )
    image_out = join_call(sc, dq_own, dkv_own, dq_got, dkv_got)[None]

    proj_grad = proj_grad_call(
        everything.reshape((groups, samples) + everything.shape[1:]), rows, width // members
    )
    return (image_out, proj_grad)


def solution(mesh):
    placed = (
        P("dp", "grp", None),
        P("dp"),
        P(),
        P(),
        P(None, "seq"),
        P(None, "seq"),
        P("seq", None),
        P(None, "seq"),
        P("dp", ("grp", "seq"), None),
        P("dp", ("grp", "seq"), None),
        P("dp", "grp", "seq"),
    )
    step = functools.partial(
        on_device,
        groups=mesh.shape["grp"],
        slots=mesh.shape["seq"],
        samples=mesh.shape["dp"],
    )
    return jax.shard_map(
        step,
        mesh=mesh,
        in_specs=placed,
        out_specs=(P("dp", "grp", "seq"), P(("grp", "dp"), "seq")),
        check_vma=False,
    )
```

```python
import functools

import jax
import jax.numpy as jnp
from jax import lax
from jax.experimental import pallas as pl
from jax.experimental.pallas import tpu as pltpu
from jax.sharding import PartitionSpec as P

f32, bf16 = jnp.float32, jnp.bfloat16
HD = 64
QB = 256
WIDE = 4
LOG2E_SCALED = 1.4426950408889634 / 8.0
VMEM_LIMIT = 50 << 20


def dot(a, b, ca, cb):
    return lax.dot_general(a, b, (((ca,), (cb,)), ((), ())), preferred_element_type=f32)


def fold8(x, op):
    return op(x.reshape(x.shape[0] // 8, 8, x.shape[1]), axis=0)


def params(limit=VMEM_LIMIT):
    return pltpu.CompilerParams(vmem_limit_bytes=limit)


def cost(flops, nbytes, trans=0):
    return pl.CostEstimate(flops=int(flops), bytes_accessed=int(nbytes), transcendentals=int(trans))


def full_spec(shape):
    return pl.BlockSpec(shape, lambda i, *_: (0,) * len(shape))


def halves(blk):
    lane = lax.broadcasted_iota(jnp.int32, blk.shape, 1)
    zero = jnp.zeros_like(blk)
    return jnp.where(lane < HD, blk, zero), jnp.where(lane >= HD, blk, zero)


def column(row):
    return jnp.transpose(jnp.broadcast_to(row, (128, row.shape[1])))


def pack_kernel(pairs, qkv_ref, cot_ref, out_ref):
    for p in range(pairs):
        for e in range(2):
            col = p * 384 + e * 192
            out_ref[e, p] = jnp.concatenate(
                [
                    qkv_ref[:, col : col + 64],
                    cot_ref[:, p * 128 + e * 64 : p * 128 + e * 64 + 64],
                    qkv_ref[:, col + 64 : col + 192],
                ],
                axis=1,
            )


def pack_call(qkv, cot):
    rows = qkv.shape[0]
    pairs = 4
    steps = qkv.shape[1] // (384 * pairs)
    return pl.pallas_call(
        functools.partial(pack_kernel, pairs),
        grid=(steps,),
        in_specs=[
            pl.BlockSpec((rows, 384 * pairs), lambda i: (0, i)),
            pl.BlockSpec((rows, 128 * pairs), lambda i: (0, i)),
        ],
        out_specs=pl.BlockSpec((2, pairs, rows, 256), lambda i: (0, i, 0, 0)),
        out_shape=jax.ShapeDtypeStruct((2, steps * pairs, rows, 256), bf16),
        compiler_params=params(60 << 20),
        cost_estimate=cost(0, 4 * qkv.size),
        name="pack_heads",
    )(qkv, cot)


def scores_kernel(first, kt, sc_ref, qd_ref, kv_ref, *refs):
    e_refs, dp_refs, st_ref, s_scr, m_scr = refs[0:2], refs[2:4], refs[4], refs[5], refs[6]
    i = pl.program_id(0)
    count = pl.num_programs(0)
    keys = kv_ref.shape[0]
    total = qd_ref.shape[0] // QB
    tiles = keys // kt
    half = tiles // 2
    start = sc_ref[0] * QB

    def block(j):
        at = lax.rem(first + j + sc_ref[0], total)
        return halves(qd_ref[pl.ds(pl.multiple_of(at * QB, QB), QB), :])

    def keys_of(t):
        return kv_ref[pl.ds(pl.multiple_of(lax.rem(start + t * kt, keys), kt), kt), :]

    def scores(t, q, mx):
        s = dot(keys_of(t), q, 1, 1)
        s_scr[t * kt : (t + 1) * kt, :] = s
        return jnp.maximum(mx, fold8(s, jnp.max))

    neg = jnp.full((8, QB), -jnp.inf, f32)

    @pl.when(i == 0)
    def _():
        q = block(0)[0]
        mx = neg
        for t in range(tiles):
            mx = scores(t, q, mx)
        m_scr[...] = mx

    m = jnp.max(m_scr[...], axis=0, keepdims=True)
    d = block(i)[1]
    q_next = block(jnp.minimum(i + 1, count - 1))[0]
    mx = neg
    l = acc = jnp.zeros((8, QB), f32)
    for t in range(tiles):
        rows = slice((t % half) * kt, (t % half + 1) * kt)
        e = jnp.exp2((s_scr[t * kt : (t + 1) * kt, :] - m) * LOG2E_SCALED)
        dp = dot(keys_of(t), d, 1, 1).astype(bf16)
        e_refs[t // half][0, rows, :] = e.astype(bf16)
        dp_refs[t // half][0, rows, :] = dp
        l = l + fold8(e, jnp.sum)
        acc = acc + fold8(e * dp.astype(f32), jnp.sum)
        mx = scores(t, q_next, mx)
    m_scr[...] = mx
    row = lax.broadcasted_iota(jnp.int32, (8, QB), 0)
    st_ref[...] = jnp.where(
        row == 0,
        m,
        jnp.where(
            row == 1, jnp.sum(l, axis=0, keepdims=True), jnp.sum(acc, axis=0, keepdims=True)
        ),
    )


def scores_call(sc, joint, first, blocks):
    tokens = joint.shape[0]
    part = tokens // 2
    big = pltpu.HBM((blocks, part, QB), bf16)
    e_o, e_n, dp_o, dp_n, st = pl.pallas_call(
        functools.partial(scores_kernel, first, 256),
        grid_spec=pltpu.PrefetchScalarGridSpec(
            num_scalar_prefetch=1,
            grid=(blocks,),
            in_specs=[
                pl.BlockSpec((tokens, 128), lambda i, sc: (0, 0)),
                pl.BlockSpec((tokens, 128), lambda i, sc: (0, 1)),
            ],
            out_specs=[pl.BlockSpec((1, part, QB), lambda i, sc: (i, 0, 0))] * 4
            + [pl.BlockSpec((8, QB), lambda i, sc: (0, i))],
            scratch_shapes=[pltpu.VMEM((tokens, QB), f32), pltpu.VMEM((8, QB), f32)],
        ),
        out_shape=[big] * 4 + [jax.ShapeDtypeStruct((8, blocks * QB), f32)],
        compiler_params=params(24 << 20),
        cost_estimate=cost(8 * blocks * QB * tokens * 128, 4 * blocks * tokens * QB),
        name="image_scores",
    )(sc, joint, joint)
    return (e_o, dp_o), (e_n, dp_n), st


def text_kernel(
    sc_ref, joint_ref, text_ref, st_ref, sent_in, dkv_ref, row_ref, dq_ref, sent_ref, s_scr, e_scr, dp_scr, gt_scr, sems
):
    tokens = joint_ref.shape[0]
    kt = 256
    tiles = tokens // kt
    wide = WIDE * QB
    tq, td = halves(text_ref[:, 0:128])
    tkv = text_ref[:, 128:256]
    tk_t = jnp.transpose(tkv.astype(f32))[0:HD, :].astype(bf16)

    def rows_of(t):
        return slice(t * kt, (t + 1) * kt)

    def masked(s):
        key = lax.broadcasted_iota(jnp.int32, s.shape, 0)
        return jnp.where(key < sc_ref[1], s, jnp.float32(-1e30))

    def stretch(i):
        at = lax.rem(i * wide + sc_ref[0] * QB, tokens)
        c = slice(i * wide, (i + 1) * wide)
        q, d = halves(joint_ref[pl.ds(pl.multiple_of(at, wide), wide), 0:128])
        s = masked(dot(tkv, q, 1, 1))
        m_img, l_img, d_img = st_ref[0:1, c], st_ref[1:2, c], st_ref[2:3, c]
        m = jnp.maximum(m_img, jnp.max(s, axis=0, keepdims=True))
        a = jnp.exp2((m_img - m) * LOG2E_SCALED)
        e = jnp.exp2((s - m) * LOG2E_SCALED)
        dp = dot(tkv, d, 1, 1).astype(bf16).astype(f32)
        r = 1.0 / (a * l_img + jnp.sum(e, axis=0, keepdims=True))
        delta = (a * d_img + jnp.sum(e * dp, axis=0, keepdims=True)) * r
        probs = e * r
        ds = (probs * (dp - delta)).astype(bf16)
        dq_ref[:, c] = dot(tk_t, ds, 1, 0) * 0.125
        row = lax.broadcasted_iota(jnp.int32, (8, wide), 0)
        row_ref[:, c] = jnp.where(row == 0, delta, a * r)
        return dot(probs.astype(bf16), d, 1, 0) + dot(ds, q * 0.125, 1, 0)

    mx = jnp.full((8, QB), -jnp.inf, f32)
    for t in range(tiles):
        s = dot(joint_ref[rows_of(t), 128:256], tq, 1, 1)
        s_scr[rows_of(t), :] = s
        mx = jnp.maximum(mx, fold8(s, jnp.max))
    st = masked(dot(tkv, tq, 1, 1))
    m = jnp.max(jnp.maximum(mx, fold8(st, jnp.max)), axis=0, keepdims=True)
    total = stretch(0)
    l = acc = jnp.zeros((8, QB), f32)

    def weigh(s, kv, l, acc):
        e = jnp.exp2((s - m) * LOG2E_SCALED)
        dp = dot(kv, td, 1, 1).astype(bf16)
        return e.astype(bf16), dp, l + fold8(e, jnp.sum), acc + fold8(e * dp.astype(f32), jnp.sum)

    for t in range(tiles):
        e, dp, l, acc = weigh(s_scr[rows_of(t), :], joint_ref[rows_of(t), 128:256], l, acc)
        e_scr[rows_of(t), :] = e
        dp_scr[rows_of(t), :] = dp
    et, dpt, l, acc = weigh(st, tkv, l, acc)
    total += stretch(1)
    r = 1.0 / jnp.sum(l, axis=0, keepdims=True)
    delta = jnp.sum(acc, axis=0, keepdims=True) * r
    tq8 = tq * 0.125

    def third(e, dp, k_t):
        probs = e.astype(f32) * r
        ds = (probs * (dp.astype(f32) - delta)).astype(bf16)
        return dot(probs.astype(bf16), td, 1, 0) + dot(ds, tq8, 1, 0), dot(k_t, ds, 1, 0)

    more, dq = third(et, dpt, tk_t)
    total += more
    for t in range(tiles):
        k_t = jnp.transpose(joint_ref[rows_of(t), 128:256].astype(f32))[0:HD, :].astype(bf16)
        dkv, more = third(e_scr[rows_of(t), :], dp_scr[rows_of(t), :], k_t)
        dkv_ref[rows_of(t), :] = dkv.astype(bf16)
        dq += more
    for i in range(2, tokens // wide):
        total += stretch(i)
    gt_scr[0:HD, :] = (dq * 0.125).astype(bf16)
    gt_scr[HD:, :] = jnp.transpose(total).astype(bf16)
    members, depth, _ = sent_ref.shape
    copies = [
        pltpu.make_async_copy(gt_scr, sent_ref.at[n, depth - 3 * HD :, :], sems.at[n])
        for n in range(members)
    ]
    for copy in copies:
        copy.start()
    for copy in copies:
        copy.wait()


def text_call(sc, joint, text, stats, sent):
    tokens = joint.shape[0]
    rows = text.shape[0]
    shapes = [(tokens, 128), (8, tokens), (HD, tokens)]
    return pl.pallas_call(
        text_kernel,
        grid_spec=pltpu.PrefetchScalarGridSpec(
            num_scalar_prefetch=1,
            grid=(1,),
            in_specs=[
                full_spec(joint.shape),
                full_spec(text.shape),
                full_spec(stats.shape),
                pl.BlockSpec(memory_space=pl.ANY),
            ],
            out_specs=[full_spec(x) for x in shapes] + [pl.BlockSpec(memory_space=pl.ANY)],
            scratch_shapes=[
                pltpu.VMEM((tokens, QB), f32),
                pltpu.VMEM((tokens, QB), bf16),
                pltpu.VMEM((tokens, QB), bf16),
                pltpu.VMEM((3 * HD, rows), bf16),
                pltpu.SemaphoreType.DMA((sent.shape[0],)),
            ],
        ),
        out_shape=[
            pltpu.HBM(shapes[0], bf16),
            jax.ShapeDtypeStruct(shapes[1], f32),
            jax.ShapeDtypeStruct(shapes[2], f32),
            pltpu.HBM(sent.shape, bf16),
        ],
        input_output_aliases={4: 3},
        compiler_params=params(40 << 20),
        cost_estimate=cost(1, 1),
        name="text_rows",
    )(sc, joint, text, stats, sent)


def grads_kernel(parts, groups, done, *refs):
    pairs = refs[1 : 1 + 2 * parts]
    rest = refs[1 + 2 * parts :]
    qd_refs, rest = rest[:groups], rest[groups:]
    row_ref, kv_ref, dkv_in = rest[:3]
    if done:
        dq_in, dq_text, dkv_ref, dq_ref, acc = rest[3:]
    else:
        dkv_ref, acc = rest[3:]
    i = pl.program_id(0)
    k_t = jnp.transpose(kv_ref[...].astype(f32))[0:HD, :].astype(bf16)
    dkv = dkv_in[...].astype(f32)

    @pl.when(i == 0)
    def _():
        acc[...] = dq_in[...] if done else jnp.zeros_like(acc)

    tiles = [(e, dp, n) for e, dp in zip(pairs[::2], pairs[1::2]) for n in range(e.shape[0])]
    per = len(tiles) // groups
    for at, (e_ref, dp_ref, n) in enumerate(tiles):
        c = slice(at * QB, (at + 1) * QB)
        probs = e_ref[n].astype(f32) * row_ref[1:2, c]
        ds = (probs * (dp_ref[n].astype(f32) - row_ref[0:1, c])).astype(bf16)
        q, d = halves(qd_refs[at // per][(at % per) * QB : (at % per + 1) * QB, :])
        dkv = dkv + dot(probs.astype(bf16), d, 1, 0) + dot(ds, q * 0.125, 1, 0)
        acc[:, c] += dot(k_t, ds, 1, 0)
    dkv_ref[...] = dkv.astype(dkv_ref.dtype)
    if done:

        @pl.when(i == pl.num_programs(0) - 1)
        def _():
            dq_ref[...] = (acc[...] * 0.125 + dq_text[...]).astype(bf16)


def grads_call(sc, pairs, row, joint, dkv_in, dq_in, dq_text, part, own_keys, last, size):
    tokens = joint.shape[0]
    queries = sum(x.shape[0] for x in pairs[::2]) * QB
    half = tokens // 2
    groups = queries // half
    all_blocks = tokens // size
    key_blocks = all_blocks // 2
    whole = dkv_in.shape[0] == tokens
    done = dq_in is not None
    parts = len(pairs) // 2

    def key_at(i, sc):
        shift = key_blocks if own_keys else 0
        return lax.rem(i + shift + lax.div(sc[0], size // QB), all_blocks)

    dq_shape = (HD, queries)
    in_specs = [pl.BlockSpec((x.shape[0], size, QB), lambda i, sc: (0, i, 0)) for x in pairs]
    for n in range(part, part + groups):
        in_specs.append(
            pl.BlockSpec(
                (half, 128), lambda i, sc, n=n: (lax.rem(n + lax.div(sc[0], half // QB), 2), 0)
            )
        )
    in_specs += [
        pl.BlockSpec((8, queries), lambda i, sc: (0, part)),
        pl.BlockSpec((size, 128), lambda i, sc: (key_at(i, sc), 1)),
        pl.BlockSpec((size, 128), lambda i, sc: (key_at(i, sc) if whole else i, 0)),
    ]
    args = [far(x) for x in pairs] + [joint] * groups + [row, joint, dkv_in]
    out_shape = [
        jax.ShapeDtypeStruct((half, 128), bf16 if last else f32),
        jax.ShapeDtypeStruct(dq_shape, bf16 if done else f32),
    ]
    scratch = []
    if done:
        in_specs += [pl.BlockSpec(dq_shape, lambda i, sc: (0, part))] * 2
        args += [dq_in, dq_text]
        scratch = [pltpu.VMEM(dq_shape, f32)]
    return pl.pallas_call(
        functools.partial(grads_kernel, parts, groups, done),
        grid_spec=pltpu.PrefetchScalarGridSpec(
            num_scalar_prefetch=1,
            grid=(key_blocks,),
            in_specs=in_specs,
            out_specs=[pl.BlockSpec((size, 128), lambda i, sc: (i, 0)), full_spec(dq_shape)],
            scratch_shapes=scratch,
        ),
        out_shape=out_shape,
        compiler_params=params(24 << 20),
        cost_estimate=cost(1, 1),
        name="image_grads",
    )(sc, *args)


def project_kernel(sc_ref, tf_ref, w_ref, cot_ref, own_ref, other_ref, feat_ref):
    qkv = dot(tf_ref[...], w_ref[...], 1, 0).astype(bf16)
    heads = []
    for e in range(2):
        heads.append(
            jnp.concatenate(
                [
                    qkv[:, e * 192 : e * 192 + 64],
                    cot_ref[:, e * 64 : e * 64 + 64],
                    qkv[:, e * 192 + 64 : e * 192 + 192],
                ],
                axis=1,
            )
        )
    flag = jnp.zeros(heads[0].shape, jnp.int32) + sc_ref[2]
    own_ref[...] = jnp.where(flag == 0, heads[0], heads[1])
    other_ref[...] = jnp.where(flag == 0, heads[1], heads[0])
    members, depth, lanes = feat_ref.shape
    rows = tf_ref.shape[0]
    parts = depth // rows
    for n in range(members):
        for f in range(parts):
            at = (n * parts + f) * lanes
            feat_ref[n, f * rows : (f + 1) * rows, :] = tf_ref[:, at : at + lanes]


def project_call(sc, tf, w, cot, members):
    rows, width = tf.shape
    feat = (members, rows * width // (members * 256), 256)
    sent = (members, feat[1] + 3 * HD, 256)
    out = jax.ShapeDtypeStruct((rows, 256), bf16)
    return pl.pallas_call(
        project_kernel,
        grid_spec=pltpu.PrefetchScalarGridSpec(
            num_scalar_prefetch=1,
            grid=(1,),
            in_specs=[full_spec(tf.shape), full_spec(w.shape), full_spec(cot.shape)],
            out_specs=[full_spec(out.shape)] * 2 + [full_spec(feat)],
        ),
        out_shape=[out, out, pltpu.HBM(sent, bf16)],
        compiler_params=params(16 << 20),
        cost_estimate=cost(2 * tf.size * w.shape[1], 2 * w.size),
        name="text_projection",
    )(sc, tf, w, cot)


def join_kernel(sc_ref, dq_ref, dkv_ref, dq_got, dkv_got, out_ref):
    def rows(dq, dkv):
        return jnp.concatenate([jnp.transpose(dq[...].astype(f32)).astype(bf16), dkv[...]], axis=1)

    own, got = rows(dq_ref, dkv_ref), rows(dq_got, dkv_got)

    @pl.when(sc_ref[2] == 0)
    def _():
        out_ref[...] = jnp.concatenate([own, got], axis=1)

    @pl.when(sc_ref[2] != 0)
    def _():
        out_ref[...] = jnp.concatenate([got, own], axis=1)


def join_call(sc, dq, dkv, dq_got, dkv_got):
    tokens = dkv.shape[0]
    dq_spec = pl.BlockSpec((HD, 512), lambda i, sc: (0, i))
    dkv_spec = pl.BlockSpec((512, 128), lambda i, sc: (i, 0))
    return pl.pallas_call(
        join_kernel,
        grid_spec=pltpu.PrefetchScalarGridSpec(
            num_scalar_prefetch=1,
            grid=(tokens // 512,),
            in_specs=[dq_spec, dkv_spec, dq_spec, dkv_spec],
            out_specs=pl.BlockSpec((512, 384), lambda i, sc: (i, 0)),
        ),
        out_shape=jax.ShapeDtypeStruct((tokens, 384), bf16),
        compiler_params=params(16 << 20),
        cost_estimate=cost(0, 4 * tokens * 384),
        name="join_heads",
    )(sc, dq, dkv, dq_got, dkv_got)


def proj_grad_kernel(rows, all_ref, out_ref):
    groups, samples, _, lanes = all_ref.shape
    parts = out_ref.shape[0] // lanes
    for f in range(parts):
        total = None
        for b in range(samples):
            gt = jnp.concatenate([all_ref[h, b, parts * rows :, :] for h in range(groups)], axis=0)
            for p in range(groups):
                tf = all_ref[p, b, f * rows : (f + 1) * rows, :]
                term = dot(tf, gt[:, p * rows : (p + 1) * rows], 0, 1)
                total = term if total is None else total + term
        out_ref[f * lanes : (f + 1) * lanes, :] = total


def proj_grad_call(everything, rows, width):
    out = jax.ShapeDtypeStruct((width, 384), f32)
    return pl.pallas_call(
        functools.partial(proj_grad_kernel, rows),
        grid=(1,),
        in_specs=[full_spec(everything.shape)],
        out_specs=full_spec(out.shape),
        out_shape=out,
        compiler_params=params(),
        cost_estimate=cost(4 * everything.size * 384, 2 * everything.size),
        name="projection_grad",
    )(everything)


def far(x):
    return pltpu.with_memory_space_constraint(x, pltpu.HBM)


def rms_norm(values_in, norm_scale):
    mean_sq = jnp.mean(values_in * values_in, axis=-1, keepdims=True)
    return values_in * lax.rsqrt(mean_sq + 1e-06) * norm_scale


def on_device(
    text_states,
    text_lengths,
    norm_gain,
    final_gain,
    wi_gate,
    wi_up,
    wo_weight,
    text_proj,
    image_qkv,
    image_cot,
    text_cot,
    groups,
    slots,
    samples,
):
    grp = lax.axis_index("grp")
    slot = lax.axis_index("seq")
    half_tokens = image_qkv.shape[1] * slots
    half_blocks = half_tokens // QB
    blocks = groups * half_blocks
    flip = [(0, 1), (1, 0)]
    sc = jnp.stack(
        [(1 - grp) * half_blocks, text_lengths[0], grp, (1 - grp) * (half_blocks // WIDE)]
    ).astype(jnp.int32)

    packed = pack_call(image_qkv[0], image_cot[0])
    packed = packed.reshape(groups * slots, image_qkv.shape[1], 256)
    joint = lax.all_to_all(packed, ("grp", "seq"), 0, 0, tiled=True)
    joint = joint.reshape(groups * half_tokens, 256)

    states = text_states[0]
    normed = rms_norm(states.astype(f32), norm_gain).astype(bf16)
    gate_act = jnp.dot(normed, wi_gate, preferred_element_type=f32)
    up_act = jnp.dot(normed, wi_up, preferred_element_type=f32)
    hidden = (jax.nn.gelu(gate_act, approximate=True) * up_act).astype(bf16)
    ffn = jnp.dot(hidden, wo_weight, preferred_element_type=f32).astype(bf16)
    rows, width = states.shape
    few = rows // slots
    ffn, joint = lax.optimization_barrier((ffn, joint))
    terms = lax.all_to_all(ffn.reshape(slots, few, width), "seq", 0, 0, tiled=True)
    far_a, near_a, st_a = scores_call(sc, joint, 0, half_blocks)
    mine = lax.dynamic_slice_in_dim(states, slot * few, few, axis=0).astype(f32)
    encoded = mine + jnp.sum(terms.astype(f32), axis=0)
    final_rows = rms_norm(encoded, final_gain).astype(bf16)
    spread = jnp.broadcast_to(final_rows[None], (slots, few, width))
    spread, joint_b, st_a = lax.optimization_barrier((spread, joint, st_a))
    text_final = lax.all_to_all(spread, "seq", 0, 0, tiled=True).reshape(rows, width)
    far_b, near_b, st_b = scores_call(sc, joint_b, half_blocks, half_blocks)

    members = groups * samples
    own, other, sent = project_call(sc, text_final, text_proj, text_cot[0], members)
    got = lax.ppermute(other, "grp", flip)
    text = jnp.where(
        grp == 0, jnp.concatenate([own, got], axis=0), jnp.concatenate([got, own], axis=0)
    )
    stats = jnp.concatenate([st_a, st_b], axis=1)
    dkv0, row, dq_text, sent = text_call(sc, joint, text, stats, sent)
    sent, row = lax.optimization_barrier((sent, row))
    everything = lax.all_to_all(sent, ("grp", "dp"), 0, 0, tiled=True)

    dkv_other, dq_all = grads_call(
        sc, far_a + far_b, row, joint, dkv0, None, None, 0, False, True, QB
    )
    dkv_got = lax.ppermute(dkv_other, "grp", flip)
    dkv2, dq_other = grads_call(
        sc, near_a, row, joint, dkv0, dq_all, dq_text, 0, True, False, 2 * QB
    )
    dq_got = lax.ppermute(dq_other, "grp", flip)
    dkv_own, dq_own = grads_call(
        sc, near_b, row, joint, dkv2, dq_all, dq_text, 1, True, True, 2 * QB
    )
    image_out = join_call(sc, dq_own, dkv_own, dq_got, dkv_got)[None]

    proj_grad = proj_grad_call(
        everything.reshape((groups, samples) + everything.shape[1:]), rows, width // members
    )
    return (image_out, proj_grad)


def solution(mesh):
    placed = (
        P("dp", "grp", None),
        P("dp"),
        P(),
        P(),
        P(None, "seq"),
        P(None, "seq"),
        P("seq", None),
        P(None, "seq"),
        P("dp", ("grp", "seq"), None),
        P("dp", ("grp", "seq"), None),
        P("dp", "grp", "seq"),
    )
    step = functools.partial(
        on_device,
        groups=mesh.shape["grp"],
        slots=mesh.shape["seq"],
        samples=mesh.shape["dp"],
    )
    return jax.shard_map(
        step,
        mesh=mesh,
        in_specs=placed,
        out_specs=(P("dp", "grp", "seq"), P(("grp", "dp"), "seq")),
        check_vma=False,
    )
```

```python
import functools

import jax
import jax.numpy as jnp
from jax import lax
from jax.experimental import pallas as pl
from jax.experimental.pallas import tpu as pltpu
from jax.sharding import PartitionSpec as P

f32, bf16 = jnp.float32, jnp.bfloat16
HD = 64
QB = 256
WIDE = 4
LOG2E_SCALED = 1.4426950408889634 / 8.0
VMEM_LIMIT = 50 << 20


def dot(a, b, ca, cb):
    return lax.dot_general(a, b, (((ca,), (cb,)), ((), ())), preferred_element_type=f32)


def fold8(x, op):
    return op(x.reshape(x.shape[0] // 8, 8, x.shape[1]), axis=0)


def params(limit=VMEM_LIMIT):
    return pltpu.CompilerParams(vmem_limit_bytes=limit)


def cost(flops, nbytes, trans=0):
    return pl.CostEstimate(flops=int(flops), bytes_accessed=int(nbytes), transcendentals=int(trans))


def full_spec(shape):
    return pl.BlockSpec(shape, lambda i, *_: (0,) * len(shape))


def halves(blk):
    lane = lax.broadcasted_iota(jnp.int32, blk.shape, 1)
    zero = jnp.zeros_like(blk)
    return jnp.where(lane < HD, blk, zero), jnp.where(lane >= HD, blk, zero)


def column(row):
    return jnp.transpose(jnp.broadcast_to(row, (128, row.shape[1])))


def pack_kernel(pairs, qkv_ref, cot_ref, out_ref):
    for p in range(pairs):
        for e in range(2):
            col = p * 384 + e * 192
            out_ref[e, p] = jnp.concatenate(
                [
                    qkv_ref[:, col : col + 64],
                    cot_ref[:, p * 128 + e * 64 : p * 128 + e * 64 + 64],
                    qkv_ref[:, col + 64 : col + 192],
                ],
                axis=1,
            )


def pack_call(qkv, cot):
    rows = qkv.shape[0]
    pairs = 8
    steps = qkv.shape[1] // (384 * pairs)
    return pl.pallas_call(
        functools.partial(pack_kernel, pairs),
        grid=(steps,),
        in_specs=[
            pl.BlockSpec((rows, 384 * pairs), lambda i: (0, i)),
            pl.BlockSpec((rows, 128 * pairs), lambda i: (0, i)),
        ],
        out_specs=pl.BlockSpec((2, pairs, rows, 256), lambda i: (0, i, 0, 0)),
        out_shape=jax.ShapeDtypeStruct((2, steps * pairs, rows, 256), bf16),
        compiler_params=params(60 << 20),
        cost_estimate=cost(0, 4 * qkv.size),
        name="pack_heads",
    )(qkv, cot)


def scores_kernel(first, kt, sc_ref, qd_ref, kv_ref, *refs):
    e_refs, dp_refs, st_ref, s_scr, m_scr = refs[0:2], refs[2:4], refs[4], refs[5], refs[6]
    i = pl.program_id(0)
    count = pl.num_programs(0)
    keys = kv_ref.shape[0]
    total = qd_ref.shape[0] // QB
    tiles = keys // kt
    half = tiles // 2
    start = sc_ref[0] * QB

    def block(j):
        at = lax.rem(first + j + sc_ref[0], total)
        return halves(qd_ref[pl.ds(pl.multiple_of(at * QB, QB), QB), :])

    def keys_of(t):
        return kv_ref[pl.ds(pl.multiple_of(lax.rem(start + t * kt, keys), kt), kt), :]

    def scores(t, q, mx):
        s = dot(keys_of(t), q, 1, 1)
        s_scr[t * kt : (t + 1) * kt, :] = s
        return jnp.maximum(mx, fold8(s, jnp.max))

    neg = jnp.full((8, QB), -jnp.inf, f32)

    @pl.when(i == 0)
    def _():
        q = block(0)[0]
        mx = neg
        for t in range(tiles):
            mx = scores(t, q, mx)
        m_scr[...] = mx

    m = jnp.max(m_scr[...], axis=0, keepdims=True)
    d = block(i)[1]
    q_next = block(jnp.minimum(i + 1, count - 1))[0]
    mx = neg
    l = acc = jnp.zeros((8, QB), f32)
    for t in range(tiles):
        rows = slice((t % half) * kt, (t % half + 1) * kt)
        e = jnp.exp2((s_scr[t * kt : (t + 1) * kt, :] - m) * LOG2E_SCALED)
        dp = dot(keys_of(t), d, 1, 1).astype(bf16)
        e_refs[t // half][0, rows, :] = e.astype(bf16)
        dp_refs[t // half][0, rows, :] = dp
        l = l + fold8(e, jnp.sum)
        acc = acc + fold8(e * dp.astype(f32), jnp.sum)
        mx = scores(t, q_next, mx)
    m_scr[...] = mx
    row = lax.broadcasted_iota(jnp.int32, (8, QB), 0)
    st_ref[...] = jnp.where(
        row == 0,
        m,
        jnp.where(
            row == 1, jnp.sum(l, axis=0, keepdims=True), jnp.sum(acc, axis=0, keepdims=True)
        ),
    )


def scores_call(sc, joint, first, blocks):
    tokens = joint.shape[0]
    part = tokens // 2
    big = pltpu.HBM((blocks, part, QB), bf16)
    e_o, e_n, dp_o, dp_n, st = pl.pallas_call(
        functools.partial(scores_kernel, first, 256),
        grid_spec=pltpu.PrefetchScalarGridSpec(
            num_scalar_prefetch=1,
            grid=(blocks,),
            in_specs=[
                pl.BlockSpec((tokens, 128), lambda i, sc: (0, 0)),
                pl.BlockSpec((tokens, 128), lambda i, sc: (0, 1)),
            ],
            out_specs=[pl.BlockSpec((1, part, QB), lambda i, sc: (i, 0, 0))] * 4
            + [pl.BlockSpec((8, QB), lambda i, sc: (0, i))],
            scratch_shapes=[pltpu.VMEM((tokens, QB), f32), pltpu.VMEM((8, QB), f32)],
        ),
        out_shape=[big] * 4 + [jax.ShapeDtypeStruct((8, blocks * QB), f32)],
        compiler_params=params(24 << 20),
        cost_estimate=cost(8 * blocks * QB * tokens * 128, 4 * blocks * tokens * QB),
        name="image_scores",
    )(sc, joint, joint)
    return (e_o, dp_o), (e_n, dp_n), st


def text_kernel(
    sc_ref, joint_ref, text_ref, st_ref, sent_in, dkv_ref, row_ref, dq_ref, sent_ref, s_scr, e_scr, dp_scr, gt_scr, sems
):
    tokens = joint_ref.shape[0]
    kt = 256
    tiles = tokens // kt
    wide = WIDE * QB
    tq, td = halves(text_ref[:, 0:128])
    tkv = text_ref[:, 128:256]
    tk_t = jnp.transpose(tkv.astype(f32))[0:HD, :].astype(bf16)

    def rows_of(t):
        return slice(t * kt, (t + 1) * kt)

    def masked(s):
        key = lax.broadcasted_iota(jnp.int32, s.shape, 0)
        return jnp.where(key < sc_ref[1], s, jnp.float32(-1e30))

    def stretch(i):
        at = lax.rem(i * wide + sc_ref[0] * QB, tokens)
        c = slice(i * wide, (i + 1) * wide)
        q, d = halves(joint_ref[pl.ds(pl.multiple_of(at, wide), wide), 0:128])
        s = masked(dot(tkv, q, 1, 1))
        m_img, l_img, d_img = st_ref[0:1, c], st_ref[1:2, c], st_ref[2:3, c]
        m = jnp.maximum(m_img, jnp.max(s, axis=0, keepdims=True))
        a = jnp.exp2((m_img - m) * LOG2E_SCALED)
        e = jnp.exp2((s - m) * LOG2E_SCALED)
        dp = dot(tkv, d, 1, 1).astype(bf16).astype(f32)
        r = 1.0 / (a * l_img + jnp.sum(e, axis=0, keepdims=True))
        delta = (a * d_img + jnp.sum(e * dp, axis=0, keepdims=True)) * r
        probs = e * r
        ds = (probs * (dp - delta)).astype(bf16)
        dq_ref[:, c] = dot(tk_t, ds, 1, 0)
        row = lax.broadcasted_iota(jnp.int32, (8, wide), 0)
        row_ref[:, c] = jnp.where(row == 0, delta, a * r)
        return dot(probs.astype(bf16), d, 1, 0) + dot(ds, q * 0.125, 1, 0)

    mx = jnp.full((8, QB), -jnp.inf, f32)
    for t in range(tiles):
        s = dot(joint_ref[rows_of(t), 128:256], tq, 1, 1)
        s_scr[rows_of(t), :] = s
        mx = jnp.maximum(mx, fold8(s, jnp.max))
    st = masked(dot(tkv, tq, 1, 1))
    m = jnp.max(jnp.maximum(mx, fold8(st, jnp.max)), axis=0, keepdims=True)
    total = stretch(0)
    l = acc = jnp.zeros((8, QB), f32)

    def weigh(s, kv, l, acc):
        e = jnp.exp2((s - m) * LOG2E_SCALED)
        dp = dot(kv, td, 1, 1).astype(bf16)
        return e.astype(bf16), dp, l + fold8(e, jnp.sum), acc + fold8(e * dp.astype(f32), jnp.sum)

    for t in range(tiles):
        e, dp, l, acc = weigh(s_scr[rows_of(t), :], joint_ref[rows_of(t), 128:256], l, acc)
        e_scr[rows_of(t), :] = e
        dp_scr[rows_of(t), :] = dp
    et, dpt, l, acc = weigh(st, tkv, l, acc)
    total += stretch(1)
    r = 1.0 / jnp.sum(l, axis=0, keepdims=True)
    delta = jnp.sum(acc, axis=0, keepdims=True) * r
    tq8 = tq * 0.125

    def third(e, dp, k_t):
        probs = e.astype(f32) * r
        ds = (probs * (dp.astype(f32) - delta)).astype(bf16)
        return dot(probs.astype(bf16), td, 1, 0) + dot(ds, tq8, 1, 0), dot(k_t, ds, 1, 0)

    more, dq = third(et, dpt, tk_t)
    total += more
    for t in range(tiles):
        k_t = jnp.transpose(joint_ref[rows_of(t), 128:256].astype(f32))[0:HD, :].astype(bf16)
        dkv, more = third(e_scr[rows_of(t), :], dp_scr[rows_of(t), :], k_t)
        dkv_ref[rows_of(t), :] = dkv.astype(bf16)
        dq += more
    for i in range(2, tokens // wide):
        total += stretch(i)
    gt_scr[0:HD, :] = (dq * 0.125).astype(bf16)
    gt_scr[HD:, :] = jnp.transpose(total).astype(bf16)
    members, depth, _ = sent_ref.shape
    copies = [
        pltpu.make_async_copy(gt_scr, sent_ref.at[n, depth - 3 * HD :, :], sems.at[n])
        for n in range(members)
    ]
    for copy in copies:
        copy.start()
    for copy in copies:
        copy.wait()


def text_call(sc, joint, text, stats, sent):
    tokens = joint.shape[0]
    rows = text.shape[0]
    shapes = [(tokens, 128), (8, tokens), (HD, tokens)]
    return pl.pallas_call(
        text_kernel,
        grid_spec=pltpu.PrefetchScalarGridSpec(
            num_scalar_prefetch=1,
            grid=(1,),
            in_specs=[
                full_spec(joint.shape),
                full_spec(text.shape),
                full_spec(stats.shape),
                pl.BlockSpec(memory_space=pl.ANY),
            ],
            out_specs=[full_spec(x) for x in shapes] + [pl.BlockSpec(memory_space=pl.ANY)],
            scratch_shapes=[
                pltpu.VMEM((tokens, QB), f32),
                pltpu.VMEM((tokens, QB), bf16),
                pltpu.VMEM((tokens, QB), bf16),
                pltpu.VMEM((3 * HD, rows), bf16),
                pltpu.SemaphoreType.DMA((sent.shape[0],)),
            ],
        ),
        out_shape=[
            pltpu.HBM(shapes[0], bf16),
            jax.ShapeDtypeStruct(shapes[1], f32),
            jax.ShapeDtypeStruct(shapes[2], f32),
            pltpu.HBM(sent.shape, bf16),
        ],
        input_output_aliases={4: 3},
        compiler_params=params(40 << 20),
        cost_estimate=cost(1, 1),
        name="text_rows",
    )(sc, joint, text, stats, sent)


def grads_kernel(parts, groups, done, *refs):
    pairs = refs[1 : 1 + 2 * parts]
    rest = refs[1 + 2 * parts :]
    qd_refs, rest = rest[:groups], rest[groups:]
    row_ref, kv_ref, dkv_in = rest[:3]
    dq_in, dkv_ref, dq_ref = rest[3:6]
    acc = rest[6] if done else dq_ref
    i = pl.program_id(0)
    k_t = jnp.transpose(kv_ref[...].astype(f32))[0:HD, :].astype(bf16)
    dkv = dkv_in[...].astype(f32)

    @pl.when(i == 0)
    def _():
        acc[...] = dq_in[...]

    tiles = [(e, dp, n) for e, dp in zip(pairs[::2], pairs[1::2]) for n in range(e.shape[0])]
    per = len(tiles) // groups
    for at, (e_ref, dp_ref, n) in enumerate(tiles):
        c = slice(at * QB, (at + 1) * QB)
        probs = e_ref[n].astype(f32) * row_ref[1:2, c]
        ds = (probs * (dp_ref[n].astype(f32) - row_ref[0:1, c])).astype(bf16)
        q, d = halves(qd_refs[at // per][(at % per) * QB : (at % per + 1) * QB, :])
        dkv = dkv + dot(probs.astype(bf16), d, 1, 0) + dot(ds, q * 0.125, 1, 0)
        acc[:, c] += dot(k_t, ds, 1, 0)
    dkv_ref[...] = dkv.astype(dkv_ref.dtype)
    if done:

        @pl.when(i == pl.num_programs(0) - 1)
        def _():
            dq_ref[...] = (acc[...] * 0.125).astype(bf16)


def grads_call(sc, pairs, row, joint, dkv_in, dq_in, part, own_keys, last, size):
    tokens = joint.shape[0]
    queries = sum(x.shape[0] for x in pairs[::2]) * QB
    half = tokens // 2
    groups = queries // half
    all_blocks = tokens // size
    key_blocks = all_blocks // 2
    whole = dkv_in.shape[0] == tokens
    done = own_keys
    parts = len(pairs) // 2

    def key_at(i, sc):
        shift = key_blocks if own_keys else 0
        return lax.rem(i + shift + lax.div(sc[0], size // QB), all_blocks)

    dq_shape = (HD, queries)
    in_specs = [pl.BlockSpec((x.shape[0], size, QB), lambda i, sc: (0, i, 0)) for x in pairs]
    for n in range(part, part + groups):
        in_specs.append(
            pl.BlockSpec(
                (half, 128), lambda i, sc, n=n: (lax.rem(n + lax.div(sc[0], half // QB), 2), 0)
            )
        )
    in_specs += [
        pl.BlockSpec((8, queries), lambda i, sc: (0, part)),
        pl.BlockSpec((size, 128), lambda i, sc: (key_at(i, sc), 1)),
        pl.BlockSpec((size, 128), lambda i, sc: (key_at(i, sc) if whole else i, 0)),
    ]
    args = [far(x) for x in pairs] + [joint] * groups + [row, joint, dkv_in]
    out_shape = [
        jax.ShapeDtypeStruct((half, 128), bf16 if last else f32),
        jax.ShapeDtypeStruct(dq_shape, bf16 if done else f32),
    ]
    in_specs.append(pl.BlockSpec(dq_shape, lambda i, sc: (0, part)))
    args.append(dq_in)
    scratch = [pltpu.VMEM(dq_shape, f32)] if done else []
    return pl.pallas_call(
        functools.partial(grads_kernel, parts, groups, done),
        grid_spec=pltpu.PrefetchScalarGridSpec(
            num_scalar_prefetch=1,
            grid=(key_blocks,),
            in_specs=in_specs,
            out_specs=[pl.BlockSpec((size, 128), lambda i, sc: (i, 0)), full_spec(dq_shape)],
            scratch_shapes=scratch,
        ),
        out_shape=out_shape,
        compiler_params=params(24 << 20),
        cost_estimate=cost(1, 1),
        name="image_grads",
    )(sc, *args)


def project_kernel(
    sc_ref, tf_ref, w_ref, cot_ref, own_ref, other_ref, sent_ref, w_near, sems, w_sems
):
    members, depth, lanes = sent_ref.shape
    rows, width = tf_ref.shape
    parts = width // (members * lanes)
    count = w_sems.shape[0]
    deep = w_ref.shape[0] // count
    loads = []
    for n in range(count):
        at = pl.ds(n * deep, deep)
        loads.append(pltpu.make_async_copy(w_ref.at[at, :], w_near.at[at, :], w_sems.at[n]))
    for load in loads:
        load.start()
    copies = []
    for n in range(members * parts):
        copies.append(
            pltpu.make_async_copy(
                tf_ref.at[:, pl.ds(n * lanes, lanes)],
                sent_ref.at[n // parts, pl.ds((n % parts) * rows, rows), :],
                sems.at[n],
            )
        )
    for copy in copies:
        copy.start()
    qkv = jnp.zeros((rows, w_ref.shape[1]), f32)
    for n, load in enumerate(loads):
        load.wait()
        at = slice(n * deep, (n + 1) * deep)
        qkv += dot(tf_ref[:, at], w_near[at, :], 1, 0)
    qkv = qkv.astype(bf16)
    heads = []
    for e in range(2):
        heads.append(
            jnp.concatenate(
                [
                    qkv[:, e * 192 : e * 192 + 64],
                    cot_ref[:, e * 64 : e * 64 + 64],
                    qkv[:, e * 192 + 64 : e * 192 + 192],
                ],
                axis=1,
            )
        )
    flag = jnp.zeros(heads[0].shape, jnp.int32) + sc_ref[2]
    own_ref[...] = jnp.where(flag == 0, heads[0], heads[1])
    other_ref[...] = jnp.where(flag == 0, heads[1], heads[0])
    for copy in copies:
        copy.wait()


def project_call(sc, tf, w, cot, members):
    rows, width = tf.shape
    sent = (members, rows * width // (members * 256) + 3 * HD, 256)
    out = jax.ShapeDtypeStruct((rows, 256), bf16)
    vmem = pl.BlockSpec(memory_space=pltpu.VMEM)
    return pl.pallas_call(
        project_kernel,
        in_specs=[
            pl.BlockSpec(memory_space=pltpu.SMEM),
            vmem,
            pl.BlockSpec(memory_space=pl.ANY),
            vmem,
        ],
        out_specs=[vmem, vmem, pl.BlockSpec(memory_space=pl.ANY)],
        out_shape=[out, out, pltpu.HBM(sent, bf16)],
        scratch_shapes=[
            pltpu.VMEM(w.shape, w.dtype),
            pltpu.SemaphoreType.DMA((width // 256,)),
            pltpu.SemaphoreType.DMA((4,)),
        ],
        compiler_params=params(16 << 20),
        cost_estimate=cost(2 * tf.size * w.shape[1], 2 * w.size),
        name="text_projection",
    )(sc, tf, far(w), cot)


def join_kernel(sc_ref, dq_ref, dkv_ref, dq_got, dkv_got, out_ref):
    def rows(dq, dkv):
        return jnp.concatenate([jnp.transpose(dq[...].astype(f32)).astype(bf16), dkv[...]], axis=1)

    own, got = rows(dq_ref, dkv_ref), rows(dq_got, dkv_got)

    @pl.when(sc_ref[2] == 0)
    def _():
        out_ref[...] = jnp.concatenate([own, got], axis=1)

    @pl.when(sc_ref[2] != 0)
    def _():
        out_ref[...] = jnp.concatenate([got, own], axis=1)


def join_call(sc, dq, dkv, dq_got, dkv_got):
    tokens = dkv.shape[0]
    dq_spec = pl.BlockSpec((HD, 512), lambda i, sc: (0, i))
    dkv_spec = pl.BlockSpec((512, 128), lambda i, sc: (i, 0))
    return pl.pallas_call(
        join_kernel,
        grid_spec=pltpu.PrefetchScalarGridSpec(
            num_scalar_prefetch=1,
            grid=(tokens // 512,),
            in_specs=[dq_spec, dkv_spec, dq_spec, dkv_spec],
            out_specs=pl.BlockSpec((512, 384), lambda i, sc: (i, 0)),
        ),
        out_shape=jax.ShapeDtypeStruct((tokens, 384), bf16),
        compiler_params=params(16 << 20),
        cost_estimate=cost(0, 4 * tokens * 384),
        name="join_heads",
    )(sc, dq, dkv, dq_got, dkv_got)


def proj_grad_kernel(rows, *refs):
    out_ref = refs[-1]
    groups, _, depth, lanes = refs[0].shape
    parts = out_ref.shape[0] // lanes
    grads = [
        jnp.concatenate([ref[h, 0, parts * rows :, :] for ref in refs[:-1]], axis=1)
        for h in range(groups)
    ]
    grads = jnp.concatenate(grads, axis=0)
    for f in range(parts):
        at = slice(f * rows, (f + 1) * rows)
        tf = jnp.concatenate([ref[p, 0, at, :] for ref in refs[:-1] for p in range(groups)], axis=0)
        out_ref[f * lanes : (f + 1) * lanes, :] = dot(tf, grads, 0, 1)


def proj_grad_call(everything, rows, width):
    groups, samples, depth, lanes = everything.shape
    out = jax.ShapeDtypeStruct((width, 384), f32)
    return pl.pallas_call(
        functools.partial(proj_grad_kernel, rows),
        grid=(1,),
        in_specs=[
            pl.BlockSpec((groups, 1, depth, lanes), lambda i, b=b: (0, b, 0, 0))
            for b in range(samples)
        ],
        out_specs=full_spec(out.shape),
        out_shape=out,
        compiler_params=params(),
        cost_estimate=cost(1, 1),
        name="projection_grad",
    )(*([far(everything)] * samples))


def norm_kernel(terms_ref, mine_ref, gain_ref, out_ref):
    total = mine_ref[...]
    for n in range(terms_ref.shape[0]):
        total = total + terms_ref[n].astype(f32)
    mean_sq = jnp.mean(total * total, axis=-1, keepdims=True)
    rows = (total * lax.rsqrt(mean_sq + 1e-06) * gain_ref[...]).astype(bf16)
    for n in range(out_ref.shape[0]):
        out_ref[n] = rows


def norm_call(terms, mine, gain):
    shapes = [terms.shape, mine.shape, (1, gain.shape[0])]
    return pl.pallas_call(
        norm_kernel,
        grid=(1,),
        in_specs=[full_spec(x) for x in shapes],
        out_specs=full_spec(terms.shape),
        out_shape=pltpu.HBM(terms.shape, bf16),
        compiler_params=params(16 << 20),
        cost_estimate=cost(1, 1),
        name="final_norm",
    )(terms, mine, gain.reshape(1, -1))


def far(x):
    return pltpu.with_memory_space_constraint(x, pltpu.HBM)


def rms_norm(values_in, norm_scale):
    mean_sq = jnp.mean(values_in * values_in, axis=-1, keepdims=True)
    return values_in * lax.rsqrt(mean_sq + 1e-06) * norm_scale


def on_device(
    text_states,
    text_lengths,
    norm_gain,
    final_gain,
    wi_gate,
    wi_up,
    wo_weight,
    text_proj,
    image_qkv,
    image_cot,
    text_cot,
    groups,
    slots,
    samples,
):
    grp = lax.axis_index("grp")
    slot = lax.axis_index("seq")
    half_tokens = image_qkv.shape[1] * slots
    half_blocks = half_tokens // QB
    blocks = groups * half_blocks
    flip = [(0, 1), (1, 0)]
    sc = jnp.stack(
        [(1 - grp) * half_blocks, text_lengths[0], grp, (1 - grp) * (half_blocks // WIDE)]
    ).astype(jnp.int32)

    packed = pack_call(image_qkv[0], image_cot[0])
    packed = packed.reshape(groups * slots, image_qkv.shape[1], 256)
    joint = lax.all_to_all(packed, ("grp", "seq"), 0, 0, tiled=True)
    joint = joint.reshape(groups * half_tokens, 256)

    states = text_states[0]
    normed = rms_norm(states.astype(f32), norm_gain).astype(bf16)
    gate_act = jnp.dot(normed, wi_gate, preferred_element_type=f32)
    up_act = jnp.dot(normed, wi_up, preferred_element_type=f32)
    hidden = (jax.nn.gelu(gate_act, approximate=True) * up_act).astype(bf16)
    ffn = jnp.dot(hidden, wo_weight, preferred_element_type=f32).astype(bf16)
    rows, width = states.shape
    few = rows // slots
    mine = lax.dynamic_slice_in_dim(states, slot * few, few, axis=0).astype(f32)
    ffn, joint, mine = lax.optimization_barrier((ffn, joint, mine))
    terms = lax.all_to_all(ffn.reshape(slots, few, width), "seq", 0, 0, tiled=True)
    far_a, near_a, st_a = scores_call(sc, joint, 0, half_blocks)
    spread = norm_call(terms, mine, final_gain)
    spread, joint_b, st_a = lax.optimization_barrier((spread, joint, st_a))
    text_final = lax.all_to_all(spread, "seq", 0, 0, tiled=True).reshape(rows, width)
    far_b, near_b, st_b = scores_call(sc, joint_b, half_blocks, half_blocks)

    members = groups * samples
    own, other, sent = project_call(sc, text_final, text_proj, text_cot[0], members)
    got = lax.ppermute(other, "grp", flip)
    text = jnp.where(
        grp == 0, jnp.concatenate([own, got], axis=0), jnp.concatenate([got, own], axis=0)
    )
    stats = jnp.concatenate([st_a, st_b], axis=1)
    dkv0, row, dq_text, sent = text_call(sc, joint, text, stats, sent)
    sent, row = lax.optimization_barrier((sent, row))
    everything = lax.all_to_all(sent, ("grp", "dp"), 0, 0, tiled=True)

    dkv_other, dq_all = grads_call(
        sc, far_a + far_b, row, joint, far(dkv0), dq_text, 0, False, True, QB
    )
    dkv_got = lax.ppermute(dkv_other, "grp", flip)
    dkv2, dq_other = grads_call(
        sc, near_a, row, joint, far(dkv0), dq_all, 0, True, False, 2 * QB
    )
    dq_got = lax.ppermute(dq_other, "grp", flip)
    dkv_own, dq_own = grads_call(
        sc, near_b, row, joint, dkv2, dq_all, 1, True, True, 2 * QB
    )
    image_out = join_call(sc, dq_own, dkv_own, dq_got, dkv_got)[None]

    proj_grad = proj_grad_call(
        everything.reshape((groups, samples) + everything.shape[1:]), rows, width // members
    )
    return (image_out, proj_grad)


def solution(mesh):
    placed = (
        P("dp", "grp", None),
        P("dp"),
        P(),
        P(),
        P(None, "seq"),
        P(None, "seq"),
        P("seq", None),
        P(None, "seq"),
        P("dp", ("grp", "seq"), None),
        P("dp", ("grp", "seq"), None),
        P("dp", "grp", "seq"),
    )
    step = functools.partial(
        on_device,
        groups=mesh.shape["grp"],
        slots=mesh.shape["seq"],
        samples=mesh.shape["dp"],
    )
    return jax.shard_map(
        step,
        mesh=mesh,
        in_specs=placed,
        out_specs=(P("dp", "grp", "seq"), P(("grp", "dp"), "seq")),
        check_vma=False,
    )
```

```python
import functools

import jax
import jax.numpy as jnp
from jax import lax
from jax.experimental import pallas as pl
from jax.experimental.pallas import tpu as pltpu
from jax.sharding import PartitionSpec as P

f32, bf16 = jnp.float32, jnp.bfloat16
HD = 64
QB = 256
WIDE = 4
LOG2E_SCALED = 1.4426950408889634 / 8.0
VMEM_LIMIT = 50 << 20


def dot(a, b, ca, cb):
    return lax.dot_general(a, b, (((ca,), (cb,)), ((), ())), preferred_element_type=f32)


def fold8(x, op):
    return op(x.reshape(x.shape[0] // 8, 8, x.shape[1]), axis=0)


def params(limit=VMEM_LIMIT):
    return pltpu.CompilerParams(vmem_limit_bytes=limit)


def cost(flops, nbytes, trans=0):
    return pl.CostEstimate(flops=int(flops), bytes_accessed=int(nbytes), transcendentals=int(trans))


def full_spec(shape):
    return pl.BlockSpec(shape, lambda i, *_: (0,) * len(shape))


def halves(blk):
    lane = lax.broadcasted_iota(jnp.int32, blk.shape, 1)
    zero = jnp.zeros_like(blk)
    return jnp.where(lane < HD, blk, zero), jnp.where(lane >= HD, blk, zero)


def column(row):
    return jnp.transpose(jnp.broadcast_to(row, (128, row.shape[1])))


def pack_kernel(pairs, qkv_ref, cot_ref, out_ref):
    for p in range(pairs):
        for e in range(2):
            col = p * 384 + e * 192
            out_ref[e, p] = jnp.concatenate(
                [
                    qkv_ref[:, col : col + 64],
                    cot_ref[:, p * 128 + e * 64 : p * 128 + e * 64 + 64],
                    qkv_ref[:, col + 64 : col + 192],
                ],
                axis=1,
            )


def pack_call(qkv, cot):
    rows = qkv.shape[0]
    pairs = 8
    steps = qkv.shape[1] // (384 * pairs)
    return pl.pallas_call(
        functools.partial(pack_kernel, pairs),
        grid=(steps,),
        in_specs=[
            pl.BlockSpec((rows, 384 * pairs), lambda i: (0, i)),
            pl.BlockSpec((rows, 128 * pairs), lambda i: (0, i)),
        ],
        out_specs=pl.BlockSpec((2, pairs, rows, 256), lambda i: (0, i, 0, 0)),
        out_shape=jax.ShapeDtypeStruct((2, steps * pairs, rows, 256), bf16),
        compiler_params=params(60 << 20),
        cost_estimate=cost(0, 4 * qkv.size),
        name="pack_heads",
    )(qkv, cot)


def scores_kernel(first, kt, sc_ref, qd_ref, kv_ref, *refs):
    e_refs, dp_refs, st_ref, s_scr, m_scr = refs[0:2], refs[2:4], refs[4], refs[5], refs[6]
    i = pl.program_id(0)
    count = pl.num_programs(0)
    keys = kv_ref.shape[0]
    total = qd_ref.shape[0] // QB
    tiles = keys // kt
    half = tiles // 2
    start = sc_ref[0] * QB

    def block(j):
        at = lax.rem(first + j + sc_ref[0], total)
        return halves(qd_ref[pl.ds(pl.multiple_of(at * QB, QB), QB), :])

    def keys_of(t):
        return kv_ref[pl.ds(pl.multiple_of(lax.rem(start + t * kt, keys), kt), kt), :]

    def scores(t, q, mx):
        s = dot(keys_of(t), q, 1, 1)
        s_scr[t * kt : (t + 1) * kt, :] = s
        return jnp.maximum(mx, fold8(s, jnp.max))

    neg = jnp.full((8, QB), -jnp.inf, f32)

    @pl.when(i == 0)
    def _():
        q = block(0)[0]
        mx = neg
        for t in range(tiles):
            mx = scores(t, q, mx)
        m_scr[...] = mx

    m = jnp.max(m_scr[...], axis=0, keepdims=True)
    d = block(i)[1]
    q_next = block(jnp.minimum(i + 1, count - 1))[0]
    mx = neg
    l = acc = jnp.zeros((8, QB), f32)
    for t in range(tiles):
        rows = slice((t % half) * kt, (t % half + 1) * kt)
        e = jnp.exp2((s_scr[t * kt : (t + 1) * kt, :] - m) * LOG2E_SCALED)
        dp = dot(keys_of(t), d, 1, 1).astype(bf16)
        e_refs[t // half][0, rows, :] = e.astype(bf16)
        dp_refs[t // half][0, rows, :] = dp
        l = l + fold8(e, jnp.sum)
        acc = acc + fold8(e * dp.astype(f32), jnp.sum)
        mx = scores(t, q_next, mx)
    m_scr[...] = mx
    row = lax.broadcasted_iota(jnp.int32, (8, QB), 0)
    st_ref[...] = jnp.where(
        row == 0,
        m,
        jnp.where(
            row == 1, jnp.sum(l, axis=0, keepdims=True), jnp.sum(acc, axis=0, keepdims=True)
        ),
    )


def scores_call(sc, joint, first, blocks):
    tokens = joint.shape[0]
    part = tokens // 2
    big = pltpu.HBM((blocks, part, QB), bf16)
    e_o, e_n, dp_o, dp_n, st = pl.pallas_call(
        functools.partial(scores_kernel, first, 256),
        grid_spec=pltpu.PrefetchScalarGridSpec(
            num_scalar_prefetch=1,
            grid=(blocks,),
            in_specs=[
                pl.BlockSpec((tokens, 128), lambda i, sc: (0, 0)),
                pl.BlockSpec((tokens, 128), lambda i, sc: (0, 1)),
            ],
            out_specs=[pl.BlockSpec((1, part, QB), lambda i, sc: (i, 0, 0))] * 4
            + [pl.BlockSpec((8, QB), lambda i, sc: (0, i))],
            scratch_shapes=[pltpu.VMEM((tokens, QB), f32), pltpu.VMEM((8, QB), f32)],
        ),
        out_shape=[big] * 4 + [jax.ShapeDtypeStruct((8, blocks * QB), f32)],
        compiler_params=params(24 << 20),
        cost_estimate=cost(8 * blocks * QB * tokens * 128, 4 * blocks * tokens * QB),
        name="image_scores",
    )(sc, joint, joint)
    return (e_o, dp_o), (e_n, dp_n), st


def text_kernel(
    sc_ref, joint_ref, text_ref, st_ref, kt_ref, sent_in, dkv_ref, row_ref, dq_ref, sent_ref, s_scr, e_scr, dp_scr, gt_scr, sems
):
    tokens = joint_ref.shape[0]
    kt = 256
    tiles = tokens // kt
    wide = WIDE * QB
    tq, td = halves(text_ref[:, 0:128])
    tkv = text_ref[:, 128:256]
    tk_t = jnp.transpose(tkv.astype(f32))[0:HD, :].astype(bf16)

    def rows_of(t):
        return slice(t * kt, (t + 1) * kt)

    def masked(s):
        key = lax.broadcasted_iota(jnp.int32, s.shape, 0)
        return jnp.where(key < sc_ref[1], s, jnp.float32(-1e30))

    def stretch(i):
        at = lax.rem(i * wide + sc_ref[0] * QB, tokens)
        c = slice(i * wide, (i + 1) * wide)
        q, d = halves(joint_ref[pl.ds(pl.multiple_of(at, wide), wide), 0:128])
        s = masked(dot(tkv, q, 1, 1))
        m_img, l_img, d_img = st_ref[0:1, c], st_ref[1:2, c], st_ref[2:3, c]
        m = jnp.maximum(m_img, jnp.max(s, axis=0, keepdims=True))
        a = jnp.exp2((m_img - m) * LOG2E_SCALED)
        e = jnp.exp2((s - m) * LOG2E_SCALED)
        dp = dot(tkv, d, 1, 1).astype(bf16).astype(f32)
        r = 1.0 / (a * l_img + jnp.sum(e, axis=0, keepdims=True))
        delta = (a * d_img + jnp.sum(e * dp, axis=0, keepdims=True)) * r
        probs = e * r
        ds = (probs * (dp - delta)).astype(bf16)
        dq_ref[:, c] = dot(tk_t, ds, 1, 0)
        row = lax.broadcasted_iota(jnp.int32, (8, wide), 0)
        row_ref[:, c] = jnp.where(row == 0, delta, a * r)
        return dot(probs.astype(bf16), d, 1, 0) + dot(ds, q * 0.125, 1, 0)

    mx = jnp.full((8, QB), -jnp.inf, f32)
    for t in range(tiles):
        s = dot(joint_ref[rows_of(t), 128:256], tq, 1, 1)
        s_scr[rows_of(t), :] = s
        mx = jnp.maximum(mx, fold8(s, jnp.max))
    st = masked(dot(tkv, tq, 1, 1))
    m = jnp.max(jnp.maximum(mx, fold8(st, jnp.max)), axis=0, keepdims=True)
    total = stretch(0)
    l = acc = jnp.zeros((8, QB), f32)

    def weigh(s, kv, l, acc):
        e = jnp.exp2((s - m) * LOG2E_SCALED)
        dp = dot(kv, td, 1, 1).astype(bf16)
        return e.astype(bf16), dp, l + fold8(e, jnp.sum), acc + fold8(e * dp.astype(f32), jnp.sum)

    for t in range(tiles):
        e, dp, l, acc = weigh(s_scr[rows_of(t), :], joint_ref[rows_of(t), 128:256], l, acc)
        e_scr[rows_of(t), :] = e
        dp_scr[rows_of(t), :] = dp
    et, dpt, l, acc = weigh(st, tkv, l, acc)
    total += stretch(1)
    r = 1.0 / jnp.sum(l, axis=0, keepdims=True)
    delta = jnp.sum(acc, axis=0, keepdims=True) * r
    tq8 = tq * 0.125

    def third(e, dp, k_t):
        probs = e.astype(f32) * r
        ds = (probs * (dp.astype(f32) - delta)).astype(bf16)
        return dot(probs.astype(bf16), td, 1, 0) + dot(ds, tq8, 1, 0), dot(k_t, ds, 1, 0)

    more, dq = third(et, dpt, tk_t)
    total += more
    for t in range(tiles):
        dkv, more = third(e_scr[rows_of(t), :], dp_scr[rows_of(t), :], kt_ref[:, rows_of(t)])
        dkv_ref[rows_of(t), :] = dkv.astype(bf16)
        dq += more
    for i in range(2, tokens // wide):
        total += stretch(i)
    gt_scr[0:HD, :] = (dq * 0.125).astype(bf16)
    gt_scr[HD:, :] = jnp.transpose(total).astype(bf16)
    members, depth, _ = sent_ref.shape
    copies = [
        pltpu.make_async_copy(gt_scr, sent_ref.at[n, depth - 3 * HD :, :], sems.at[n])
        for n in range(members)
    ]
    for copy in copies:
        copy.start()
    for copy in copies:
        copy.wait()


def text_call(sc, joint, text, stats, keys_t, sent):
    tokens = joint.shape[0]
    rows = text.shape[0]
    shapes = [(tokens, 128), (8, tokens), (HD, tokens)]
    return pl.pallas_call(
        text_kernel,
        grid_spec=pltpu.PrefetchScalarGridSpec(
            num_scalar_prefetch=1,
            grid=(1,),
            in_specs=[
                full_spec(joint.shape),
                full_spec(text.shape),
                full_spec(stats.shape),
                full_spec(keys_t.shape),
                pl.BlockSpec(memory_space=pl.ANY),
            ],
            out_specs=[full_spec(x) for x in shapes] + [pl.BlockSpec(memory_space=pl.ANY)],
            scratch_shapes=[
                pltpu.VMEM((tokens, QB), f32),
                pltpu.VMEM((tokens, QB), bf16),
                pltpu.VMEM((tokens, QB), bf16),
                pltpu.VMEM((3 * HD, rows), bf16),
                pltpu.SemaphoreType.DMA((sent.shape[0],)),
            ],
        ),
        out_shape=[
            pltpu.HBM(shapes[0], bf16),
            jax.ShapeDtypeStruct(shapes[1], f32),
            jax.ShapeDtypeStruct(shapes[2], f32),
            pltpu.HBM(sent.shape, bf16),
        ],
        input_output_aliases={5: 3},
        compiler_params=params(40 << 20),
        cost_estimate=cost(1, 1),
        name="text_rows",
    )(sc, joint, text, stats, keys_t, sent)


def grads_kernel(parts, groups, done, *refs):
    pairs = refs[1 : 1 + 2 * parts]
    rest = refs[1 + 2 * parts :]
    qd_refs, rest = rest[:groups], rest[groups:]
    row_ref, kt_ref, dkv_in = rest[:3]
    dq_in, dkv_ref, dq_ref = rest[3:6]
    acc = rest[6] if done else dq_ref
    i = pl.program_id(0)
    k_t = kt_ref[...]
    dkv = dkv_in[...].astype(f32)

    @pl.when(i == 0)
    def _():
        acc[...] = dq_in[...]

    tiles = [(e, dp, n) for e, dp in zip(pairs[::2], pairs[1::2]) for n in range(e.shape[0])]
    per = len(tiles) // groups
    for at, (e_ref, dp_ref, n) in enumerate(tiles):
        c = slice(at * QB, (at + 1) * QB)
        probs = e_ref[n].astype(f32) * row_ref[1:2, c]
        ds = (probs * (dp_ref[n].astype(f32) - row_ref[0:1, c])).astype(bf16)
        q, d = halves(qd_refs[at // per][(at % per) * QB : (at % per + 1) * QB, :])
        dkv = dkv + dot(probs.astype(bf16), d, 1, 0) + dot(ds, q * 0.125, 1, 0)
        acc[:, c] += dot(k_t, ds, 1, 0)
    dkv_ref[...] = dkv.astype(dkv_ref.dtype)
    if done:

        @pl.when(i == pl.num_programs(0) - 1)
        def _():
            dq_ref[...] = (acc[...] * 0.125).astype(bf16)


def grads_call(sc, pairs, row, joint, keys_t, dkv_in, dq_in, part, own_keys, last, size):
    tokens = joint.shape[0]
    queries = sum(x.shape[0] for x in pairs[::2]) * QB
    half = tokens // 2
    groups = queries // half
    all_blocks = tokens // size
    key_blocks = all_blocks // 2
    whole = dkv_in.shape[0] == tokens
    done = own_keys
    parts = len(pairs) // 2

    def key_at(i, sc):
        shift = key_blocks if own_keys else 0
        return lax.rem(i + shift + lax.div(sc[0], size // QB), all_blocks)

    dq_shape = (HD, queries)
    in_specs = [pl.BlockSpec((x.shape[0], size, QB), lambda i, sc: (0, i, 0)) for x in pairs]
    for n in range(part, part + groups):
        in_specs.append(
            pl.BlockSpec(
                (half, 128), lambda i, sc, n=n: (lax.rem(n + lax.div(sc[0], half // QB), 2), 0)
            )
        )
    in_specs += [
        pl.BlockSpec((8, queries), lambda i, sc: (0, part)),
        pl.BlockSpec((HD, size), lambda i, sc: (0, key_at(i, sc))),
        pl.BlockSpec((size, 128), lambda i, sc: (key_at(i, sc) if whole else i, 0)),
    ]
    args = [far(x) for x in pairs] + [joint] * groups + [row, keys_t, dkv_in]
    out_shape = [
        jax.ShapeDtypeStruct((half, 128), bf16 if last else f32),
        jax.ShapeDtypeStruct(dq_shape, bf16 if done else f32),
    ]
    in_specs.append(pl.BlockSpec(dq_shape, lambda i, sc: (0, part)))
    args.append(dq_in)
    scratch = [pltpu.VMEM(dq_shape, f32)] if done else []
    return pl.pallas_call(
        functools.partial(grads_kernel, parts, groups, done),
        grid_spec=pltpu.PrefetchScalarGridSpec(
            num_scalar_prefetch=1,
            grid=(key_blocks,),
            in_specs=in_specs,
            out_specs=[pl.BlockSpec((size, 128), lambda i, sc: (i, 0)), full_spec(dq_shape)],
            scratch_shapes=scratch,
        ),
        out_shape=out_shape,
        compiler_params=params(24 << 20),
        cost_estimate=cost(1, 1),
        name="image_grads",
    )(sc, *args)


def project_kernel(sc_ref, tf_ref, w_ref, cot_ref, own_ref, other_ref, w_near, w_sems):
    rows = tf_ref.shape[0]
    count = w_sems.shape[0]
    deep = w_ref.shape[0] // count
    loads = []
    for n in range(count):
        at = pl.ds(n * deep, deep)
        loads.append(pltpu.make_async_copy(w_ref.at[at, :], w_near.at[at, :], w_sems.at[n]))
    for load in loads:
        load.start()
    qkv = jnp.zeros((rows, w_ref.shape[1]), f32)
    for n, load in enumerate(loads):
        load.wait()
        at = slice(n * deep, (n + 1) * deep)
        qkv += dot(tf_ref[:, at], w_near[at, :], 1, 0)
    qkv = qkv.astype(bf16)
    heads = []
    for e in range(2):
        heads.append(
            jnp.concatenate(
                [
                    qkv[:, e * 192 : e * 192 + 64],
                    cot_ref[:, e * 64 : e * 64 + 64],
                    qkv[:, e * 192 + 64 : e * 192 + 192],
                ],
                axis=1,
            )
        )
    flag = jnp.zeros(heads[0].shape, jnp.int32) + sc_ref[2]
    own_ref[...] = jnp.where(flag == 0, heads[0], heads[1])
    other_ref[...] = jnp.where(flag == 0, heads[1], heads[0])


def project_call(sc, tf, w, cot):
    rows = tf.shape[0]
    out = jax.ShapeDtypeStruct((rows, 256), bf16)
    vmem = pl.BlockSpec(memory_space=pltpu.VMEM)
    return pl.pallas_call(
        project_kernel,
        in_specs=[
            pl.BlockSpec(memory_space=pltpu.SMEM),
            vmem,
            pl.BlockSpec(memory_space=pl.ANY),
            vmem,
        ],
        out_specs=[vmem, vmem],
        out_shape=[out, out],
        scratch_shapes=[pltpu.VMEM(w.shape, w.dtype), pltpu.SemaphoreType.DMA((4,))],
        compiler_params=params(16 << 20),
        cost_estimate=cost(2 * tf.size * w.shape[1], 2 * w.size),
        name="text_projection",
    )(sc, tf, far(w), cot)


def aside_kernel(tf_ref, joint_ref, kt_ref, kt_far, sent_ref, sems, kt_sem):
    members, _, lanes = sent_ref.shape
    rows, width = tf_ref.shape
    parts = width // (members * lanes)
    copies = []
    for n in range(members * parts):
        copies.append(
            pltpu.make_async_copy(
                tf_ref.at[:, pl.ds(n * lanes, lanes)],
                sent_ref.at[n // parts, pl.ds((n % parts) * rows, rows), :],
                sems.at[n],
            )
        )
    for copy in copies:
        copy.start()
    for t in range(joint_ref.shape[0] // QB):
        at = slice(t * QB, (t + 1) * QB)
        kt_ref[:, at] = jnp.transpose(joint_ref[at, 128:256].astype(f32))[0:HD, :].astype(bf16)
    kt_copy = pltpu.make_async_copy(kt_ref, kt_far, kt_sem)
    kt_copy.start()
    for copy in copies:
        copy.wait()
    kt_copy.wait()


def aside_call(tf, joint, members):
    rows, width = tf.shape
    sent = (members, rows * width // (members * 256) + 3 * HD, 256)
    vmem = pl.BlockSpec(memory_space=pltpu.VMEM)
    return pl.pallas_call(
        aside_kernel,
        in_specs=[vmem, vmem],
        out_specs=[vmem] + [pl.BlockSpec(memory_space=pl.ANY)] * 2,
        out_shape=[
            jax.ShapeDtypeStruct((HD, joint.shape[0]), bf16),
            pltpu.HBM((HD, joint.shape[0]), bf16),
            pltpu.HBM(sent, bf16),
        ],
        scratch_shapes=[
            pltpu.SemaphoreType.DMA((width // 256,)),
            pltpu.SemaphoreType.DMA,
        ],
        compiler_params=params(16 << 20),
        cost_estimate=cost(1, 1),
        name="keys_aside",
    )(tf, joint)


def join_kernel(sc_ref, dq_ref, dkv_ref, dq_got, dkv_got, out_ref):
    def rows(dq, dkv):
        return jnp.concatenate([jnp.transpose(dq[...].astype(f32)).astype(bf16), dkv[...]], axis=1)

    own, got = rows(dq_ref, dkv_ref), rows(dq_got, dkv_got)

    @pl.when(sc_ref[2] == 0)
    def _():
        out_ref[...] = jnp.concatenate([own, got], axis=1)

    @pl.when(sc_ref[2] != 0)
    def _():
        out_ref[...] = jnp.concatenate([got, own], axis=1)


def join_call(sc, dq, dkv, dq_got, dkv_got):
    tokens = dkv.shape[0]
    dq_spec = pl.BlockSpec((HD, 512), lambda i, sc: (0, i))
    dkv_spec = pl.BlockSpec((512, 128), lambda i, sc: (i, 0))
    return pl.pallas_call(
        join_kernel,
        grid_spec=pltpu.PrefetchScalarGridSpec(
            num_scalar_prefetch=1,
            grid=(tokens // 512,),
            in_specs=[dq_spec, dkv_spec, dq_spec, dkv_spec],
            out_specs=pl.BlockSpec((512, 384), lambda i, sc: (i, 0)),
        ),
        out_shape=jax.ShapeDtypeStruct((tokens, 384), bf16),
        compiler_params=params(16 << 20),
        cost_estimate=cost(0, 4 * tokens * 384),
        name="join_heads",
    )(sc, dq, dkv, dq_got, dkv_got)


def proj_grad_kernel(rows, *refs):
    out_ref = refs[-1]
    groups, _, depth, lanes = refs[0].shape
    parts = out_ref.shape[0] // lanes
    grads = [
        jnp.concatenate([ref[h, 0, parts * rows :, :] for ref in refs[:-1]], axis=1)
        for h in range(groups)
    ]
    grads = jnp.concatenate(grads, axis=0)
    for f in range(parts):
        at = slice(f * rows, (f + 1) * rows)
        tf = jnp.concatenate([ref[p, 0, at, :] for ref in refs[:-1] for p in range(groups)], axis=0)
        out_ref[f * lanes : (f + 1) * lanes, :] = dot(tf, grads, 0, 1)


def proj_grad_call(everything, rows, width):
    groups, samples, depth, lanes = everything.shape
    out = jax.ShapeDtypeStruct((width, 384), f32)
    return pl.pallas_call(
        functools.partial(proj_grad_kernel, rows),
        grid=(1,),
        in_specs=[
            pl.BlockSpec((groups, 1, depth, lanes), lambda i, b=b: (0, b, 0, 0))
            for b in range(samples)
        ],
        out_specs=full_spec(out.shape),
        out_shape=out,
        compiler_params=params(),
        cost_estimate=cost(1, 1),
        name="projection_grad",
    )(*([far(everything)] * samples))


def norm_kernel(terms_ref, mine_ref, gain_ref, out_ref):
    total = mine_ref[...]
    for n in range(terms_ref.shape[0]):
        total = total + terms_ref[n].astype(f32)
    mean_sq = jnp.mean(total * total, axis=-1, keepdims=True)
    rows = (total * lax.rsqrt(mean_sq + 1e-06) * gain_ref[...]).astype(bf16)
    for n in range(out_ref.shape[0]):
        out_ref[n] = rows


def norm_call(terms, mine, gain):
    shapes = [terms.shape, mine.shape, (1, gain.shape[0])]
    return pl.pallas_call(
        norm_kernel,
        grid=(1,),
        in_specs=[full_spec(x) for x in shapes],
        out_specs=full_spec(terms.shape),
        out_shape=pltpu.HBM(terms.shape, bf16),
        compiler_params=params(16 << 20),
        cost_estimate=cost(1, 1),
        name="final_norm",
    )(terms, mine, gain.reshape(1, -1))


def far(x):
    return pltpu.with_memory_space_constraint(x, pltpu.HBM)


def rms_norm(values_in, norm_scale):
    mean_sq = jnp.mean(values_in * values_in, axis=-1, keepdims=True)
    return values_in * lax.rsqrt(mean_sq + 1e-06) * norm_scale


def on_device(
    text_states,
    text_lengths,
    norm_gain,
    final_gain,
    wi_gate,
    wi_up,
    wo_weight,
    text_proj,
    image_qkv,
    image_cot,
    text_cot,
    groups,
    slots,
    samples,
):
    grp = lax.axis_index("grp")
    slot = lax.axis_index("seq")
    half_tokens = image_qkv.shape[1] * slots
    half_blocks = half_tokens // QB
    blocks = groups * half_blocks
    flip = [(0, 1), (1, 0)]
    sc = jnp.stack(
        [(1 - grp) * half_blocks, text_lengths[0], grp, (1 - grp) * (half_blocks // WIDE)]
    ).astype(jnp.int32)

    packed = pack_call(image_qkv[0], image_cot[0])
    packed = packed.reshape(groups * slots, image_qkv.shape[1], 256)
    joint = lax.all_to_all(packed, ("grp", "seq"), 0, 0, tiled=True)
    joint = joint.reshape(groups * half_tokens, 256)

    states = text_states[0]
    normed = rms_norm(states.astype(f32), norm_gain).astype(bf16)
    gate_act = jnp.dot(normed, wi_gate, preferred_element_type=f32)
    up_act = jnp.dot(normed, wi_up, preferred_element_type=f32)
    hidden = (jax.nn.gelu(gate_act, approximate=True) * up_act).astype(bf16)
    ffn = jnp.dot(hidden, wo_weight, preferred_element_type=f32).astype(bf16)
    rows, width = states.shape
    few = rows // slots
    mine = lax.dynamic_slice_in_dim(states, slot * few, few, axis=0).astype(f32)
    ffn, joint, mine, sc = lax.optimization_barrier((ffn, joint, mine, sc))
    terms = lax.all_to_all(ffn.reshape(slots, few, width), "seq", 0, 0, tiled=True)
    far_a, near_a, st_a = scores_call(sc, joint, 0, half_blocks)
    spread = norm_call(terms, mine, final_gain)
    spread, joint_b, st_a = lax.optimization_barrier((spread, joint, st_a))
    text_final = lax.all_to_all(spread, "seq", 0, 0, tiled=True).reshape(rows, width)
    far_b, near_b, st_b = scores_call(sc, joint_b, half_blocks, half_blocks)

    members = groups * samples
    own, other = project_call(sc, text_final, text_proj, text_cot[0])
    got = lax.ppermute(other, "grp", flip)
    own, text_final = lax.optimization_barrier((own, text_final))
    keys_near, keys_t, sent = aside_call(text_final, joint, members)
    keys_t = far(keys_t)
    text = jnp.where(
        grp == 0, jnp.concatenate([own, got], axis=0), jnp.concatenate([got, own], axis=0)
    )
    stats = jnp.concatenate([st_a, st_b], axis=1)
    dkv0, row, dq_text, sent = text_call(sc, joint, text, stats, keys_near, sent)
    sent, row = lax.optimization_barrier((sent, row))
    everything = lax.all_to_all(sent, ("grp", "dp"), 0, 0, tiled=True)

    dkv_other, dq_all = grads_call(
        sc, far_a + far_b, row, joint, keys_t, far(dkv0), dq_text, 0, False, True, QB
    )
    dkv_got = lax.ppermute(dkv_other, "grp", flip)
    dkv2, dq_other = grads_call(
        sc, near_a, row, joint, keys_t, far(dkv0), dq_all, 0, True, False, 2 * QB
    )
    dq_got = lax.ppermute(dq_other, "grp", flip)
    dkv_own, dq_own = grads_call(
        sc, near_b, row, joint, keys_t, dkv2, dq_all, 1, True, True, 2 * QB
    )
    image_out = join_call(sc, dq_own, dkv_own, dq_got, dkv_got)[None]

    proj_grad = proj_grad_call(
        everything.reshape((groups, samples) + everything.shape[1:]), rows, width // members
    )
    return (image_out, proj_grad)


def solution(mesh):
    placed = (
        P("dp", "grp", None),
        P("dp"),
        P(),
        P(),
        P(None, "seq"),
        P(None, "seq"),
        P("seq", None),
        P(None, "seq"),
        P("dp", ("grp", "seq"), None),
        P("dp", ("grp", "seq"), None),
        P("dp", "grp", "seq"),
    )
    step = functools.partial(
        on_device,
        groups=mesh.shape["grp"],
        slots=mesh.shape["seq"],
        samples=mesh.shape["dp"],
    )
    return jax.shard_map(
        step,
        mesh=mesh,
        in_specs=placed,
        out_specs=(P("dp", "grp", "seq"), P(("grp", "dp"), "seq")),
        check_vma=False,
    )
```

```python
import functools

import jax
import jax.numpy as jnp
from jax import lax
from jax.experimental import pallas as pl
from jax.experimental.pallas import tpu as pltpu
from jax.sharding import PartitionSpec as P

f32, bf16 = jnp.float32, jnp.bfloat16
HD = 64
QB = 256
WIDE = 4
LOG2E_SCALED = 1.4426950408889634 / 8.0
VMEM_LIMIT = 50 << 20


def dot(a, b, ca, cb):
    return lax.dot_general(a, b, (((ca,), (cb,)), ((), ())), preferred_element_type=f32)


def fold8(x, op):
    return op(x.reshape(x.shape[0] // 8, 8, x.shape[1]), axis=0)


def params(limit=VMEM_LIMIT):
    return pltpu.CompilerParams(vmem_limit_bytes=limit)


def cost(flops, nbytes, trans=0):
    return pl.CostEstimate(flops=int(flops), bytes_accessed=int(nbytes), transcendentals=int(trans))


def full_spec(shape):
    return pl.BlockSpec(shape, lambda i, *_: (0,) * len(shape))


def halves(blk):
    lane = lax.broadcasted_iota(jnp.int32, blk.shape, 1)
    zero = jnp.zeros_like(blk)
    return jnp.where(lane < HD, blk, zero), jnp.where(lane >= HD, blk, zero)


def column(row):
    return jnp.transpose(jnp.broadcast_to(row, (128, row.shape[1])))


def pack_kernel(pairs, qkv_ref, cot_ref, out_ref):
    for p in range(pairs):
        for e in range(2):
            col = p * 384 + e * 192
            out_ref[e, p] = jnp.concatenate(
                [
                    qkv_ref[:, col : col + 64],
                    cot_ref[:, p * 128 + e * 64 : p * 128 + e * 64 + 64],
                    qkv_ref[:, col + 64 : col + 192],
                ],
                axis=1,
            )


def pack_call(qkv, cot):
    rows = qkv.shape[0]
    pairs = 8
    steps = qkv.shape[1] // (384 * pairs)
    return pl.pallas_call(
        functools.partial(pack_kernel, pairs),
        grid=(steps,),
        in_specs=[
            pl.BlockSpec((rows, 384 * pairs), lambda i: (0, i)),
            pl.BlockSpec((rows, 128 * pairs), lambda i: (0, i)),
        ],
        out_specs=pl.BlockSpec((2, pairs, rows, 256), lambda i: (0, i, 0, 0)),
        out_shape=jax.ShapeDtypeStruct((2, steps * pairs, rows, 256), bf16),
        compiler_params=params(60 << 20),
        cost_estimate=cost(0, 4 * qkv.size),
        name="pack_heads",
    )(qkv, cot)


def scores_kernel(first, kt, sc_ref, qd_ref, kv_ref, *refs):
    e_refs, dp_refs, st_ref, s_scr, m_scr = refs[0:2], refs[2:4], refs[4], refs[5], refs[6]
    i = pl.program_id(0)
    count = pl.num_programs(0)
    keys = kv_ref.shape[0]
    total = qd_ref.shape[0] // QB
    tiles = keys // kt
    half = tiles // 2
    start = sc_ref[0] * QB

    def block(j):
        at = lax.rem(first + j + sc_ref[0], total)
        return halves(qd_ref[pl.ds(pl.multiple_of(at * QB, QB), QB), :])

    def keys_of(t):
        return kv_ref[pl.ds(pl.multiple_of(lax.rem(start + t * kt, keys), kt), kt), :]

    def scores(t, q, mx):
        s = dot(keys_of(t), q, 1, 1)
        s_scr[t * kt : (t + 1) * kt, :] = s
        return jnp.maximum(mx, fold8(s, jnp.max))

    neg = jnp.full((8, QB), -jnp.inf, f32)

    @pl.when(i == 0)
    def _():
        q = block(0)[0]
        mx = neg
        for t in range(tiles):
            mx = scores(t, q, mx)
        m_scr[...] = mx

    m = jnp.max(m_scr[...], axis=0, keepdims=True)
    d = block(i)[1]
    q_next = block(jnp.minimum(i + 1, count - 1))[0]
    mx = neg
    l = acc = jnp.zeros((8, QB), f32)
    for t in range(tiles):
        rows = slice((t % half) * kt, (t % half + 1) * kt)
        e = jnp.exp2((s_scr[t * kt : (t + 1) * kt, :] - m) * LOG2E_SCALED)
        dp = dot(keys_of(t), d, 1, 1).astype(bf16)
        e_refs[t // half][0, rows, :] = e.astype(bf16)
        dp_refs[t // half][0, rows, :] = dp
        l = l + fold8(e, jnp.sum)
        acc = acc + fold8(e * dp.astype(f32), jnp.sum)
        mx = scores(t, q_next, mx)
    m_scr[...] = mx
    row = lax.broadcasted_iota(jnp.int32, (8, QB), 0)
    st_ref[...] = jnp.where(
        row == 0,
        m,
        jnp.where(
            row == 1, jnp.sum(l, axis=0, keepdims=True), jnp.sum(acc, axis=0, keepdims=True)
        ),
    )


def scores_call(sc, joint, first, blocks):
    tokens = joint.shape[0]
    part = tokens // 2
    big = pltpu.HBM((blocks, part, QB), bf16)
    e_o, e_n, dp_o, dp_n, st = pl.pallas_call(
        functools.partial(scores_kernel, first, 256),
        grid_spec=pltpu.PrefetchScalarGridSpec(
            num_scalar_prefetch=1,
            grid=(blocks,),
            in_specs=[
                pl.BlockSpec((tokens, 128), lambda i, sc: (0, 0)),
                pl.BlockSpec((tokens, 128), lambda i, sc: (0, 1)),
            ],
            out_specs=[pl.BlockSpec((1, part, QB), lambda i, sc: (i, 0, 0))] * 4
            + [pl.BlockSpec((8, QB), lambda i, sc: (0, i))],
            scratch_shapes=[pltpu.VMEM((tokens, QB), f32), pltpu.VMEM((8, QB), f32)],
        ),
        out_shape=[big] * 4 + [jax.ShapeDtypeStruct((8, blocks * QB), f32)],
        compiler_params=params(24 << 20),
        cost_estimate=cost(8 * blocks * QB * tokens * 128, 4 * blocks * tokens * QB),
        name="image_scores",
    )(sc, joint, joint)
    return (e_o, dp_o), (e_n, dp_n), st


def text_kernel(
    sc_ref, joint_ref, text_ref, st_ref, kt_ref, sent_in, dkv_ref, row_ref, dq_ref, sent_ref, s_scr, e_scr, dp_scr, gt_scr, sems
):
    tokens = joint_ref.shape[0]
    kt = 256
    tiles = tokens // kt
    wide = WIDE * QB
    tq, td = halves(text_ref[:, 0:128])
    tkv = text_ref[:, 128:256]
    tk_t = jnp.transpose(tkv.astype(f32))[0:HD, :].astype(bf16)

    def rows_of(t):
        return slice(t * kt, (t + 1) * kt)

    def masked(s):
        key = lax.broadcasted_iota(jnp.int32, s.shape, 0)
        return jnp.where(key < sc_ref[1], s, jnp.float32(-1e30))

    def stretch(i):
        at = lax.rem(i * wide + sc_ref[0] * QB, tokens)
        c = slice(i * wide, (i + 1) * wide)
        q, d = halves(joint_ref[pl.ds(pl.multiple_of(at, wide), wide), 0:128])
        s = masked(dot(tkv, q, 1, 1))
        m_img, l_img, d_img = st_ref[0:1, c], st_ref[1:2, c], st_ref[2:3, c]
        m = jnp.maximum(m_img, jnp.max(s, axis=0, keepdims=True))
        a = jnp.exp2((m_img - m) * LOG2E_SCALED)
        e = jnp.exp2((s - m) * LOG2E_SCALED)
        dp = dot(tkv, d, 1, 1).astype(bf16).astype(f32)
        r = 1.0 / (a * l_img + jnp.sum(e, axis=0, keepdims=True))
        delta = (a * d_img + jnp.sum(e * dp, axis=0, keepdims=True)) * r
        probs = e * r
        ds = (probs * (dp - delta)).astype(bf16)
        dq_ref[:, c] = dot(tk_t, ds, 1, 0)
        row = lax.broadcasted_iota(jnp.int32, (8, wide), 0)
        row_ref[:, c] = jnp.where(row == 0, delta, a * r)
        return dot(probs.astype(bf16), d, 1, 0) + dot(ds, q * 0.125, 1, 0)

    mx = jnp.full((8, QB), -jnp.inf, f32)
    for t in range(tiles):
        s = dot(joint_ref[rows_of(t), 128:256], tq, 1, 1)
        s_scr[rows_of(t), :] = s
        mx = jnp.maximum(mx, fold8(s, jnp.max))
    st = masked(dot(tkv, tq, 1, 1))
    m = jnp.max(jnp.maximum(mx, fold8(st, jnp.max)), axis=0, keepdims=True)
    total = stretch(0)
    l = acc = jnp.zeros((8, QB), f32)

    def weigh(s, kv, l, acc):
        e = jnp.exp2((s - m) * LOG2E_SCALED)
        dp = dot(kv, td, 1, 1).astype(bf16)
        return e.astype(bf16), dp, l + fold8(e, jnp.sum), acc + fold8(e * dp.astype(f32), jnp.sum)

    for t in range(tiles):
        e, dp, l, acc = weigh(s_scr[rows_of(t), :], joint_ref[rows_of(t), 128:256], l, acc)
        e_scr[rows_of(t), :] = e
        dp_scr[rows_of(t), :] = dp
    et, dpt, l, acc = weigh(st, tkv, l, acc)
    total += stretch(1)
    r = 1.0 / jnp.sum(l, axis=0, keepdims=True)
    delta = jnp.sum(acc, axis=0, keepdims=True) * r
    tq8 = tq * 0.125

    def third(e, dp, k_t):
        probs = e.astype(f32) * r
        ds = (probs * (dp.astype(f32) - delta)).astype(bf16)
        return dot(probs.astype(bf16), td, 1, 0) + dot(ds, tq8, 1, 0), dot(k_t, ds, 1, 0)

    more, dq = third(et, dpt, tk_t)
    total += more
    for t in range(tiles):
        dkv, more = third(e_scr[rows_of(t), :], dp_scr[rows_of(t), :], kt_ref[:, rows_of(t)])
        dkv_ref[rows_of(t), :] = dkv.astype(bf16)
        dq += more
    for i in range(2, tokens // wide):
        total += stretch(i)
    gt_scr[0:HD, :] = (dq * 0.125).astype(bf16)
    gt_scr[HD:, :] = jnp.transpose(total).astype(bf16)
    members, depth, _ = sent_ref.shape
    copies = [
        pltpu.make_async_copy(gt_scr, sent_ref.at[n, depth - 3 * HD :, :], sems.at[n])
        for n in range(members)
    ]
    for copy in copies:
        copy.start()
    for copy in copies:
        copy.wait()


def text_call(sc, joint, text, stats, keys_t, sent):
    tokens = joint.shape[0]
    rows = text.shape[0]
    shapes = [(tokens, 128), (8, tokens), (HD, tokens)]
    return pl.pallas_call(
        text_kernel,
        grid_spec=pltpu.PrefetchScalarGridSpec(
            num_scalar_prefetch=1,
            grid=(1,),
            in_specs=[
                full_spec(joint.shape),
                full_spec(text.shape),
                full_spec(stats.shape),
                full_spec(keys_t.shape),
                pl.BlockSpec(memory_space=pl.ANY),
            ],
            out_specs=[full_spec(x) for x in shapes] + [pl.BlockSpec(memory_space=pl.ANY)],
            scratch_shapes=[
                pltpu.VMEM((tokens, QB), f32),
                pltpu.VMEM((tokens, QB), bf16),
                pltpu.VMEM((tokens, QB), bf16),
                pltpu.VMEM((3 * HD, rows), bf16),
                pltpu.SemaphoreType.DMA((sent.shape[0],)),
            ],
        ),
        out_shape=[
            pltpu.HBM(shapes[0], bf16),
            jax.ShapeDtypeStruct(shapes[1], f32),
            jax.ShapeDtypeStruct(shapes[2], f32),
            pltpu.HBM(sent.shape, bf16),
        ],
        input_output_aliases={5: 3},
        compiler_params=params(40 << 20),
        cost_estimate=cost(1, 1),
        name="text_rows",
    )(sc, joint, text, stats, keys_t, sent)


def grads_kernel(parts, groups, done, *refs):
    pairs = refs[1 : 1 + 2 * parts]
    rest = refs[1 + 2 * parts :]
    qd_refs, rest = rest[:groups], rest[groups:]
    row_ref, kt_ref, dkv_in = rest[:3]
    dq_in, dkv_ref, dq_ref = rest[3:6]
    acc = rest[6] if done else dq_ref
    i = pl.program_id(0)
    k_t = kt_ref[...]
    dkv = dkv_in[...].astype(f32)

    @pl.when(i == 0)
    def _():
        acc[...] = dq_in[...]

    tiles = [(e, dp, n) for e, dp in zip(pairs[::2], pairs[1::2]) for n in range(e.shape[0])]
    per = len(tiles) // groups
    for at, (e_ref, dp_ref, n) in enumerate(tiles):
        c = slice(at * QB, (at + 1) * QB)
        probs = e_ref[n].astype(f32) * row_ref[1:2, c]
        ds = (probs * (dp_ref[n].astype(f32) - row_ref[0:1, c])).astype(bf16)
        q, d = halves(qd_refs[at // per][(at % per) * QB : (at % per + 1) * QB, :])
        dkv = dkv + dot(probs.astype(bf16), d, 1, 0) + dot(ds, q * 0.125, 1, 0)
        acc[:, c] += dot(k_t, ds, 1, 0)
    dkv_ref[...] = dkv.astype(dkv_ref.dtype)
    if done:

        @pl.when(i == pl.num_programs(0) - 1)
        def _():
            dq_ref[...] = (acc[...] * 0.125).astype(bf16)


def grads_call(sc, pairs, row, joint, keys_t, dkv_in, dq_in, part, own_keys, last, size):
    tokens = joint.shape[0]
    queries = sum(x.shape[0] for x in pairs[::2]) * QB
    half = tokens // 2
    groups = queries // half
    all_blocks = tokens // size
    key_blocks = all_blocks // 2
    whole = dkv_in.shape[0] == tokens
    done = own_keys
    parts = len(pairs) // 2

    def key_at(i, sc):
        shift = key_blocks if own_keys else 0
        return lax.rem(i + shift + lax.div(sc[0], size // QB), all_blocks)

    dq_shape = (HD, queries)
    in_specs = [pl.BlockSpec((x.shape[0], size, QB), lambda i, sc: (0, i, 0)) for x in pairs]
    for n in range(part, part + groups):
        in_specs.append(
            pl.BlockSpec(
                (half, 128), lambda i, sc, n=n: (lax.rem(n + lax.div(sc[0], half // QB), 2), 0)
            )
        )
    in_specs += [
        pl.BlockSpec((8, queries), lambda i, sc: (0, part)),
        pl.BlockSpec((HD, size), lambda i, sc: (0, key_at(i, sc))),
        pl.BlockSpec((size, 128), lambda i, sc: (key_at(i, sc) if whole else i, 0)),
    ]
    args = [far(x) for x in pairs] + [joint] * groups + [row, keys_t, dkv_in]
    out_shape = [
        jax.ShapeDtypeStruct((half, 128), bf16 if last else f32),
        jax.ShapeDtypeStruct(dq_shape, bf16 if done else f32),
    ]
    in_specs.append(pl.BlockSpec(dq_shape, lambda i, sc: (0, part)))
    args.append(dq_in)
    scratch = [pltpu.VMEM(dq_shape, f32)] if done else []
    return pl.pallas_call(
        functools.partial(grads_kernel, parts, groups, done),
        grid_spec=pltpu.PrefetchScalarGridSpec(
            num_scalar_prefetch=1,
            grid=(key_blocks,),
            in_specs=in_specs,
            out_specs=[pl.BlockSpec((size, 128), lambda i, sc: (i, 0)), full_spec(dq_shape)],
            scratch_shapes=scratch,
        ),
        out_shape=out_shape,
        compiler_params=params(24 << 20),
        cost_estimate=cost(1, 1),
        name="image_grads",
    )(sc, *args)


def project_kernel(sc_ref, tf_ref, w_ref, cot_ref, own_ref, other_ref, w_near, w_sems):
    rows = tf_ref.shape[0]
    count = w_sems.shape[0]
    deep = w_ref.shape[0] // count
    loads = []
    for n in range(count):
        at = pl.ds(n * deep, deep)
        loads.append(pltpu.make_async_copy(w_ref.at[at, :], w_near.at[at, :], w_sems.at[n]))
    for load in loads:
        load.start()
    qkv = jnp.zeros((rows, w_ref.shape[1]), f32)
    for n, load in enumerate(loads):
        load.wait()
        at = slice(n * deep, (n + 1) * deep)
        qkv += dot(tf_ref[:, at], w_near[at, :], 1, 0)
    qkv = qkv.astype(bf16)
    heads = []
    for e in range(2):
        heads.append(
            jnp.concatenate(
                [
                    qkv[:, e * 192 : e * 192 + 64],
                    cot_ref[:, e * 64 : e * 64 + 64],
                    qkv[:, e * 192 + 64 : e * 192 + 192],
                ],
                axis=1,
            )
        )
    flag = jnp.zeros(heads[0].shape, jnp.int32) + sc_ref[2]
    own_ref[...] = jnp.where(flag == 0, heads[0], heads[1])
    other_ref[...] = jnp.where(flag == 0, heads[1], heads[0])


def project_call(sc, tf, w, cot):
    rows = tf.shape[0]
    out = jax.ShapeDtypeStruct((rows, 256), bf16)
    vmem = pl.BlockSpec(memory_space=pltpu.VMEM)
    return pl.pallas_call(
        project_kernel,
        in_specs=[
            pl.BlockSpec(memory_space=pltpu.SMEM),
            vmem,
            pl.BlockSpec(memory_space=pl.ANY),
            vmem,
        ],
        out_specs=[vmem, vmem],
        out_shape=[out, out],
        scratch_shapes=[pltpu.VMEM(w.shape, w.dtype), pltpu.SemaphoreType.DMA((4,))],
        compiler_params=params(16 << 20),
        cost_estimate=cost(2 * tf.size * w.shape[1], 2 * w.size),
        name="text_projection",
    )(sc, tf, far(w), cot)


def aside_kernel(tf_ref, joint_ref, kt_ref, kt_far, sent_ref, sems, kt_sem):
    members, _, lanes = sent_ref.shape
    rows, width = tf_ref.shape
    parts = width // (members * lanes)
    copies = []
    for n in range(members * parts):
        copies.append(
            pltpu.make_async_copy(
                tf_ref.at[:, pl.ds(n * lanes, lanes)],
                sent_ref.at[n // parts, pl.ds((n % parts) * rows, rows), :],
                sems.at[n],
            )
        )
    for copy in copies:
        copy.start()
    for t in range(joint_ref.shape[0] // QB):
        at = slice(t * QB, (t + 1) * QB)
        kt_ref[:, at] = jnp.transpose(joint_ref[at, 128:256].astype(f32))[0:HD, :].astype(bf16)
    kt_copy = pltpu.make_async_copy(kt_ref, kt_far, kt_sem)
    kt_copy.start()
    for copy in copies:
        copy.wait()
    kt_copy.wait()


def aside_call(tf, joint, members):
    rows, width = tf.shape
    sent = (members, rows * width // (members * 256) + 3 * HD, 256)
    vmem = pl.BlockSpec(memory_space=pltpu.VMEM)
    return pl.pallas_call(
        aside_kernel,
        in_specs=[vmem, vmem],
        out_specs=[vmem] + [pl.BlockSpec(memory_space=pl.ANY)] * 2,
        out_shape=[
            jax.ShapeDtypeStruct((HD, joint.shape[0]), bf16),
            pltpu.HBM((HD, joint.shape[0]), bf16),
            pltpu.HBM(sent, bf16),
        ],
        scratch_shapes=[
            pltpu.SemaphoreType.DMA((width // 256,)),
            pltpu.SemaphoreType.DMA,
        ],
        compiler_params=params(16 << 20),
        cost_estimate=cost(1, 1),
        name="keys_aside",
    )(tf, joint)


def join_kernel(sc_ref, dq_ref, dkv_ref, dq_got, dkv_got, out_ref):
    def rows(dq, dkv):
        return jnp.concatenate([jnp.transpose(dq[...].astype(f32)).astype(bf16), dkv[...]], axis=1)

    own, got = rows(dq_ref, dkv_ref), rows(dq_got, dkv_got)

    @pl.when(sc_ref[2] == 0)
    def _():
        out_ref[...] = jnp.concatenate([own, got], axis=1)

    @pl.when(sc_ref[2] != 0)
    def _():
        out_ref[...] = jnp.concatenate([got, own], axis=1)


def join_call(sc, dq, dkv, dq_got, dkv_got):
    tokens = dkv.shape[0]
    dq_spec = pl.BlockSpec((HD, 1024), lambda i, sc: (0, i))
    dkv_spec = pl.BlockSpec((1024, 128), lambda i, sc: (i, 0))
    return pl.pallas_call(
        join_kernel,
        grid_spec=pltpu.PrefetchScalarGridSpec(
            num_scalar_prefetch=1,
            grid=(tokens // 1024,),
            in_specs=[dq_spec, dkv_spec, dq_spec, dkv_spec],
            out_specs=pl.BlockSpec((1024, 384), lambda i, sc: (i, 0)),
        ),
        out_shape=jax.ShapeDtypeStruct((tokens, 384), bf16),
        compiler_params=params(16 << 20),
        cost_estimate=cost(0, 4 * tokens * 384),
        name="join_heads",
    )(sc, dq, dkv, dq_got, dkv_got)


def proj_grad_kernel(rows, *refs):
    out_ref = refs[-1]
    groups, _, depth, lanes = refs[0].shape
    parts = out_ref.shape[0] // lanes
    grads = [
        jnp.concatenate([ref[h, 0, parts * rows :, :] for ref in refs[:-1]], axis=1)
        for h in range(groups)
    ]
    grads = jnp.concatenate(grads, axis=0)
    for f in range(parts):
        at = slice(f * rows, (f + 1) * rows)
        tf = jnp.concatenate([ref[p, 0, at, :] for ref in refs[:-1] for p in range(groups)], axis=0)
        out_ref[f * lanes : (f + 1) * lanes, :] = dot(tf, grads, 0, 1)


def proj_grad_call(everything, rows, width):
    groups, samples, depth, lanes = everything.shape
    out = jax.ShapeDtypeStruct((width, 384), f32)
    return pl.pallas_call(
        functools.partial(proj_grad_kernel, rows),
        grid=(1,),
        in_specs=[
            pl.BlockSpec((groups, 1, depth, lanes), lambda i, b=b: (0, b, 0, 0))
            for b in range(samples)
        ],
        out_specs=full_spec(out.shape),
        out_shape=out,
        compiler_params=params(),
        cost_estimate=cost(1, 1),
        name="projection_grad",
    )(*([far(everything)] * samples))


def norm_kernel(terms_ref, mine_ref, gain_ref, out_ref):
    total = mine_ref[...]
    for n in range(terms_ref.shape[0]):
        total = total + terms_ref[n].astype(f32)
    mean_sq = jnp.mean(total * total, axis=-1, keepdims=True)
    rows = (total * lax.rsqrt(mean_sq + 1e-06) * gain_ref[...]).astype(bf16)
    for n in range(out_ref.shape[0]):
        out_ref[n] = rows


def norm_call(terms, mine, gain):
    shapes = [terms.shape, mine.shape, (1, gain.shape[0])]
    return pl.pallas_call(
        norm_kernel,
        grid=(1,),
        in_specs=[full_spec(x) for x in shapes],
        out_specs=full_spec(terms.shape),
        out_shape=pltpu.HBM(terms.shape, bf16),
        compiler_params=params(16 << 20),
        cost_estimate=cost(1, 1),
        name="final_norm",
    )(terms, mine, gain.reshape(1, -1))


def far(x):
    return pltpu.with_memory_space_constraint(x, pltpu.HBM)


def rms_norm(values_in, norm_scale):
    mean_sq = jnp.mean(values_in * values_in, axis=-1, keepdims=True)
    return values_in * lax.rsqrt(mean_sq + 1e-06) * norm_scale


def on_device(
    text_states,
    text_lengths,
    norm_gain,
    final_gain,
    wi_gate,
    wi_up,
    wo_weight,
    text_proj,
    image_qkv,
    image_cot,
    text_cot,
    groups,
    slots,
    samples,
):
    grp = lax.axis_index("grp")
    slot = lax.axis_index("seq")
    half_tokens = image_qkv.shape[1] * slots
    half_blocks = half_tokens // QB
    blocks = groups * half_blocks
    flip = [(0, 1), (1, 0)]
    sc = jnp.stack(
        [(1 - grp) * half_blocks, text_lengths[0], grp, (1 - grp) * (half_blocks // WIDE)]
    ).astype(jnp.int32)

    packed = pack_call(image_qkv[0], image_cot[0])
    packed = packed.reshape(groups * slots, image_qkv.shape[1], 256)
    joint = lax.all_to_all(packed, ("grp", "seq"), 0, 0, tiled=True)
    joint = joint.reshape(groups * half_tokens, 256)

    states = text_states[0]
    normed = rms_norm(states.astype(f32), norm_gain).astype(bf16)
    gate_act = jnp.dot(normed, wi_gate, preferred_element_type=f32)
    up_act = jnp.dot(normed, wi_up, preferred_element_type=f32)
    hidden = (jax.nn.gelu(gate_act, approximate=True) * up_act).astype(bf16)
    ffn = jnp.dot(hidden, wo_weight, preferred_element_type=f32).astype(bf16)
    rows, width = states.shape
    few = rows // slots
    mine = lax.dynamic_slice_in_dim(states, slot * few, few, axis=0).astype(f32)
    ffn, joint, mine, sc = lax.optimization_barrier((ffn, joint, mine, sc))
    terms = lax.all_to_all(ffn.reshape(slots, few, width), "seq", 0, 0, tiled=True)
    far_a, near_a, st_a = scores_call(sc, joint, 0, half_blocks)
    spread = norm_call(terms, mine, final_gain)
    spread, joint_b, st_a = lax.optimization_barrier((spread, joint, st_a))
    text_final = lax.all_to_all(spread, "seq", 0, 0, tiled=True).reshape(rows, width)
    far_b, near_b, st_b = scores_call(sc, joint_b, half_blocks, half_blocks)

    members = groups * samples
    own, other = project_call(sc, text_final, text_proj, text_cot[0])
    got = lax.ppermute(other, "grp", flip)
    own, text_final = lax.optimization_barrier((own, text_final))
    keys_near, keys_t, sent = aside_call(text_final, joint, members)
    keys_t = far(keys_t)
    text = jnp.where(
        grp == 0, jnp.concatenate([own, got], axis=0), jnp.concatenate([got, own], axis=0)
    )
    stats = jnp.concatenate([st_a, st_b], axis=1)
    dkv0, row, dq_text, sent = text_call(sc, joint, text, stats, keys_near, sent)
    sent, row = lax.optimization_barrier((sent, row))
    everything = lax.all_to_all(sent, ("grp", "dp"), 0, 0, tiled=True)

    dkv_other, dq_all = grads_call(
        sc, far_a + far_b, row, joint, keys_t, far(dkv0), dq_text, 0, False, True, QB
    )
    dkv_got = lax.ppermute(dkv_other, "grp", flip)
    dkv2, dq_other = grads_call(
        sc, near_a, row, joint, keys_t, far(dkv0), dq_all, 0, True, False, 2 * QB
    )
    dq_got = lax.ppermute(dq_other, "grp", flip)
    dkv_own, dq_own = grads_call(
        sc, near_b, row, joint, keys_t, dkv2, dq_all, 1, True, True, 2 * QB
    )
    image_out = join_call(sc, dq_own, dkv_own, dq_got, dkv_got)[None]

    proj_grad = proj_grad_call(
        everything.reshape((groups, samples) + everything.shape[1:]), rows, width // members
    )
    return (image_out, proj_grad)


def solution(mesh):
    placed = (
        P("dp", "grp", None),
        P("dp"),
        P(),
        P(),
        P(None, "seq"),
        P(None, "seq"),
        P("seq", None),
        P(None, "seq"),
        P("dp", ("grp", "seq"), None),
        P("dp", ("grp", "seq"), None),
        P("dp", "grp", "seq"),
    )
    step = functools.partial(
        on_device,
        groups=mesh.shape["grp"],
        slots=mesh.shape["seq"],
        samples=mesh.shape["dp"],
    )
    return jax.shard_map(
        step,
        mesh=mesh,
        in_specs=placed,
        out_specs=(P("dp", "grp", "seq"), P(("grp", "dp"), "seq")),
        check_vma=False,
    )
```
